128 devices in a mesh: dp: 16 (over x, z), group: 8 (over y, core).
Axes of the slice: x: 4, y: 4, z: 4, core: 2. Of those that a mesh axis runs over, the one named last changes fastest.
Arguments:
- acts: bfloat16 [8192, 4096], P('dp', 'group'), may hold values from -9 to 9
- grads_out: bfloat16 [8192, 16384], P('dp', 'group'), may hold values from -1 to 1
- owners: int32 [16, 16, 1], P('dp'), may hold values from 0 to 7; in each aligned block of 16 rows (0 to 15, 16 to 31, ..., all dimensions but the last counted through in order) at most 3 rows name the same one
- left_stats: float32 [16, 8, 3, 512, 512], P('dp', 'group'), may hold values from -1 to 4
- right_stats: float32 [16, 8, 3, 512, 512], P('dp', 'group'), may hold values from -1 to 4
- left_root: bfloat16 [16, 8, 3, 512, 512], P('dp', 'group'), may hold values from -1 to 3
- right_root: bfloat16 [16, 8, 3, 512, 512], P('dp', 'group'), may hold values from -1 to 3
Outputs:
- left_new: float32 [16, 8, 3, 512, 512], P('dp', 'group')
- right_new: float32 [16, 8, 3, 512, 512], P('dp', 'group')
- update: bfloat16 [256, 512, 512], P(('group', 'dp'))
The draws below stay inside these ranges and needn't reach their ends.
Inputs may be any that keep to these rules, and one draw needn't show every extreme that they name: `owners`: in the 16 rows of one dp index no owner is named more than 3 times.
All inputs are finite; a program needn't handle non-finite values.
Results may differ from the reference program's by a relative error of at most 0.029.
Values may be sent and summed in bfloat16 or wider, within the bound.
A program may use at most 192 MiB of HBM per device.

```python
import math
import jax
import jax.numpy as jnp
import numpy as np
from jax import lax

D = 4096
F = 16384
BLK = 512
TOK_DEV = 512
TOKENS = 8192
NBLK = 256
BPD = 2
ROWB = 16
CAP = 3
N_DP = 16
N_GROUP = 8


def scaled_field(key, rows, columns, along_rows, factor):
    key_scale, key_noise = jax.random.split(key)
    top = 10.0
    noise = jnp.clip(jax.random.normal(key_noise, (rows, columns), jnp.float32), -4.0, 4.0)
    spread = math.sqrt((top * top - 1.0) / (2.0 * math.log(top)))
    count = columns if along_rows == 0 else rows
    scaling = jnp.exp(jax.random.uniform(key_scale, (count,), jnp.float32) * math.log(top)) / spread
    if along_rows == 0:
        return noise * scaling[None, :] * factor
    return noise * scaling[:, None] * factor


def draw_acts(key, part):
    key = jax.random.fold_in(key, 11)
    return scaled_field(key, TOKENS, D, 0, 1.0).astype(jnp.bfloat16)


def draw_grads_out(key, part):
    key = jax.random.fold_in(key, 12)
    factor = 1.0 / math.sqrt(BLK * TOKENS)
    return scaled_field(key, TOKENS, F, 0, factor).astype(jnp.bfloat16)


def symmetric_blocks(key, low, high, off_scale):
    key_diag, key_off = jax.random.split(key)
    shape = (N_DP, N_GROUP, CAP, BLK, BLK)
    raw = jnp.clip(jax.random.normal(key_off, shape, jnp.float32), -4.0, 4.0)
    mirror = (raw + jnp.swapaxes(raw, 3, 4)) * 0.7071
    diag_vals = jnp.exp(math.log(low) + jax.random.uniform(key_diag, (N_DP, N_GROUP, CAP, BLK), jnp.float32) * math.log(high / low))
    rows_at = jax.lax.broadcasted_iota(jnp.int32, (BLK, BLK), 0)
    cols_at = jax.lax.broadcasted_iota(jnp.int32, (BLK, BLK), 1)
    identity = (rows_at == cols_at).astype(jnp.float32)
    return identity * diag_vals[..., None] + (1.0 - identity) * off_scale * mirror


def draw_left_stats(key, part):
    key = jax.random.fold_in(key, 21)
    return symmetric_blocks(key, 0.3, 3.0, 0.02)


def draw_right_stats(key, part):
    key = jax.random.fold_in(key, 22)
    return symmetric_blocks(key, 0.3, 3.0, 0.02)


def draw_left_root(key, part):
    key = jax.random.fold_in(key, 23)
    return symmetric_blocks(key, 0.5, 2.0, 0.3 / math.sqrt(BLK)).astype(jnp.bfloat16)


def draw_right_root(key, part):
    key = jax.random.fold_in(key, 24)
    return symmetric_blocks(key, 0.5, 2.0, 0.3 / math.sqrt(BLK)).astype(jnp.bfloat16)


def routed_block(own_key, own, number, rows, amount, top, reach, lean):
    sequence = jax.random.permutation(own_key, amount)
    heavy_load, common = load_shares(amount, rows * top, reach, lean, True), load_shares(amount, rows * top, reach, lean, False)
    places = jnp.arange(amount)

    def named(sizes, rotation):
        used = int((sizes > 0).sum())
        fixed = max(1, used // 4)
        moved = fixed + (places - fixed + rotation * (used - fixed)) % max(1, amount - fixed)
        return jnp.zeros((amount,), jnp.int32).at[sequence[jnp.where(places < fixed, places, moved)]].set(jnp.asarray(sizes, jnp.int32))

    sizes = jnp.where(number % 4 == 0, named(heavy_load, number // 4), named(common, number - number // 4 - 1))
    mixed = jax.random.permutation(jax.random.fold_in(own, 3), amount)
    source_of, taker = mixed[0:amount // 2 * 2:2], mixed[1:amount // 2 * 2:2]
    room = jnp.minimum(sizes[source_of] - 1, reach - sizes[taker]) // 2
    room = jnp.where((source_of == sequence[0]) | (taker == sequence[0]) | (sizes[taker] == 0), 0, jnp.maximum(room, 0))
    moved = jax.random.randint(jax.random.fold_in(own, 4), (amount // 2,), 0, 1 << 20) % (room + 1)
    sizes = sizes.at[source_of].add(-moved).at[taker].add(moved)
    items = jnp.searchsorted(jnp.cumsum(sizes), jnp.arange(rows * top), side="right").astype(jnp.int32)
    table = items.reshape(top, rows).T
    table = table[jax.random.permutation(jax.random.fold_in(own, 1), rows)]
    rotation = jax.random.randint(jax.random.fold_in(own, 2), (rows, 1), 0, top)
    return jnp.take_along_axis(table, (jnp.arange(top)[None, :] + rotation) % top, axis=1)


def load_shares(number_of, total, reach, skew, full):
    portions = [(1 << 20) // math.isqrt(standing ** skew) + 1 for standing in range(1, number_of + 1)]
    largest = reach if full else min(reach, max(-(-total // number_of), total * portions[0] // sum(portions)))
    least = 1 if total - largest >= number_of - 1 else 0
    counts, spare = [largest] + [least] * (number_of - 1), total - largest - least * (number_of - 1)
    while spare > 0:
        movable = [i for i in range(1, number_of) if counts[i] < largest] or [i for i in range(1, number_of) if counts[i] < reach]
        pool, remaining = sum([portions[i] for i in movable]), spare
        for i in movable:
            more = min(reach - counts[i], max(1, remaining * portions[i] // pool), spare)
            counts[i] = counts[i] + more
            spare = spare - more
    return np.array(counts)


def setup_inputs(seed: int = 0) -> dict:
    streams_of = jax.random.split(jax.random.key(seed), 8)
    acts = draw_acts(jax.random.fold_in(streams_of[7], 71), 0)
    grads_out = draw_grads_out(jax.random.fold_in(streams_of[7], 71), 0)
    owners_keys = jax.random.split(jax.random.fold_in(streams_of[2], 1), N_DP * ROWB // ROWB)
    owners_turns = jax.random.permutation(jax.random.fold_in(streams_of[2], 3), N_DP * ROWB // ROWB)
    owners = jax.vmap(lambda own, number: routed_block(jax.random.fold_in(streams_of[2], 2), own, number, ROWB, N_GROUP, 1, CAP, 2))(owners_keys, owners_turns).reshape((N_DP, ROWB, 1))
    left_stats = draw_left_stats(jax.random.fold_in(streams_of[7], 71), 0)
    right_stats = draw_right_stats(jax.random.fold_in(streams_of[7], 71), 0)
    left_root = draw_left_root(jax.random.fold_in(streams_of[7], 71), 0)
    right_root = draw_right_root(jax.random.fold_in(streams_of[7], 71), 0)
    return {"acts": acts, "grads_out": grads_out, "owners": owners, "left_stats": left_stats, "right_stats": right_stats, "left_root": left_root, "right_root": right_root}


STAT_DECAY = 0.9
EPSILON = 1e-06

def reference(acts, grads_out, owners, left_stats, right_stats, left_root, right_root):

    def add_part(index, accum_sum):
        act_rows = lax.dynamic_slice_in_dim(acts, index * TOK_DEV, TOK_DEV, 0).astype(jnp.float32)
        grad_rows = lax.dynamic_slice_in_dim(grads_out, index * TOK_DEV, TOK_DEV, 0).astype(jnp.float32)
        term_block = jnp.einsum('tf,td->fd', grad_rows, act_rows)
        rounded = lax.optimization_barrier(term_block.astype(jnp.bfloat16))
        return accum_sum + rounded.astype(jnp.float32)
    gradient = lax.fori_loop(0, N_DP, add_part, jnp.zeros((F, D), jnp.float32)).astype(jnp.bfloat16)
    col_blocks = D // BLK
    blocks = gradient.reshape(F // BLK, BLK, col_blocks, BLK).transpose(0, 2, 1, 3).reshape(NBLK, BLK, BLK)
    position = jnp.arange(ROWB).astype(jnp.int32)
    dp_rows = jnp.arange(N_DP).astype(jnp.int32)
    block_ids = (position[None, :] // BPD * (N_DP * BPD) + dp_rows[:, None] * BPD + position[None, :] % BPD).astype(jnp.int32)
    owner_ids = owners[:, :, 0]
    matches = owner_ids[:, :, None] == owner_ids[:, None, :]
    earlier = position[None, :] < position[:, None]
    slot_ids = lax.optimization_barrier(jnp.sum((matches & earlier[None]).astype(jnp.int32), axis=2))
    groups = jnp.arange(N_GROUP).astype(jnp.int32)
    slots = jnp.arange(CAP).astype(jnp.int32)
    selection = ((owner_ids[:, :, None, None] == groups[None, None, :, None]) & (slot_ids[:, :, None, None] == slots[None, None, None, :])).astype(jnp.float32)

    def per_row(inputs):
        chooser, row_ids, left_now, right_now, left_fourth, right_fourth = inputs
        row_blocks = blocks[row_ids].astype(jnp.float32)
        owned = jnp.einsum('kos,kab->osab', chooser, row_blocks)
        left_gram = jnp.einsum('osab,oscb->osac', owned, owned)
        right_gram = jnp.einsum('osab,osac->osbc', owned, owned)
        left_next = STAT_DECAY * left_now + (1.0 - STAT_DECAY) * left_gram
        right_next = STAT_DECAY * right_now + (1.0 - STAT_DECAY) * right_gram
        shaped = jnp.einsum('osab,osbc->osac', left_fourth.astype(jnp.float32), owned).astype(jnp.bfloat16)
        product = jnp.einsum('osab,osbc->osac', shaped.astype(jnp.float32), right_fourth.astype(jnp.float32))
        scaling = lax.rsqrt(lax.optimization_barrier(jnp.mean(product * product, axis=(2, 3), keepdims=True)) + EPSILON)
        scaled = (product * scaling).astype(jnp.bfloat16)
        returned = jnp.einsum('kos,osab->kab', chooser, scaled.astype(jnp.float32)).astype(jnp.bfloat16)
        return (left_next, right_next, returned)
    left_new, right_new, returned = lax.map(per_row, (selection, block_ids, left_stats, right_stats, left_root, right_root))
    update = jnp.zeros((NBLK, BLK, BLK), jnp.bfloat16).at[block_ids.reshape(-1)].set(returned.reshape(N_DP * ROWB, BLK, BLK))
    return (left_new, right_new, update)
```

```python
import functools

import jax
import jax.numpy as jnp
from jax import lax
from jax.experimental import pallas as pl
from jax.experimental.pallas import tpu as pltpu
from jax.sharding import PartitionSpec as P

MESH = pl.DeviceIdType.MESH
STAT_DECAY = 0.9
EPSILON = 1e-06
BLK = 512
SIDE = 4
ROUNDS = 4
PART = BLK // 4
F32 = jnp.float32
BF16 = jnp.bfloat16


def place():
    dp, group = lax.axis_index("dp"), lax.axis_index("group")
    return dp // SIDE, group // 2, lax.rem(dp, SIDE), lax.rem(group, 2)


def ring(index, step):
    return lax.rem(index + step + SIDE, SIDE)


def device(x, y, z, core):
    return (x * SIDE + z, y * 2 + core)


def remote(src, dst, send, recv, target):
    return pltpu.make_async_remote_copy(
        src_ref=src, dst_ref=dst, send_sem=send, recv_sem=recv, device_id=target, device_id_type=MESH
    )


def greet(targets):
    barrier = pltpu.get_barrier_semaphore()
    for target in targets:
        pl.semaphore_signal(barrier, inc=1, device_id=target, device_id_type=MESH)
    pl.semaphore_wait(barrier, len(targets))


def plus(*terms):
    total = terms[0].astype(F32)
    for term in terms[1:]:
        total = total + term.astype(F32)
    return total.astype(BF16)


class RingSum:
    def __init__(self, part, me, right, left, far, near, send, recv):
        self.part, self.me = part, me
        to_right = [
            (part(ring(me, 2)).at[0], far.at[0]),
            (part(ring(me, 1)).at[1], near.at[0, 1]),
            (part(ring(me, 1)).at[0], near.at[0, 0]),
        ]
        to_left = [
            (part(ring(me, 2)).at[1], far.at[1]),
            (part(ring(me, -1)).at[0], near.at[1, 0]),
            (part(ring(me, -1)).at[1], near.at[1, 1]),
        ]
        self.far, self.near = far, near
        self.copies = []
        for i in range(3):
            for j, (target, lists) in enumerate(((right, to_right), (left, to_left))):
                src, dst = lists[i]
                self.copies.append(remote(src, dst, send.at[2 * i + j], recv.at[2 * i + j], target))

    def first(self):
        for copy in self.copies[:4]:
            copy.start()

    def merge(self):
        for j, (step, half) in enumerate(((1, 0), (-1, 1))):
            self.copies[j].wait_recv()
            ref = self.part(ring(self.me, step)).at[half]
            ref[...] = plus(ref[...], self.far[j])
            self.copies[4 + j].start()

    def total(self):
        for copy in self.copies[2:]:
            copy.wait_recv()
        mine = self.part(self.me)
        return [plus(mine[half], self.near[0, half], self.near[1, half]) for half in range(2)]

    def finish(self):
        for copy in self.copies:
            copy.wait_send()


def reduce_kernel(
    acts_ref, grads_ref, all_ref,
    grads, turned, acts, parts, far1, near1, sums, far2, near2, done,
    local_sem, acts_send, acts_recv, pair_send, pair_recv,
    send1, recv1, send2, recv2, out_send, out_recv, cross_send, cross_recv,
):
    x, y, z, core = place()
    other = 1 - core
    group = y * 2 + core
    partner = device(x, y, z, other)
    along_y = [device(x, ring(y, s), z, core) for s in (1, -1, 2)]
    along_x = [device(ring(x, s), y, z, core) for s in (1, -1)]
    along_z = [device(x, y, ring(z, s), core) for s in (1, -1)]

    load_grads = pltpu.make_async_copy(grads_ref, grads, local_sem.at[0])
    load_acts = pltpu.make_async_copy(acts_ref, acts.at[core, y], local_sem.at[1])
    load_grads.start()
    load_acts.start()
    greet([partner] + along_y + along_x + along_z)

    load_acts.wait()
    own = acts.at[core, y]
    acts_out = [remote(own, own, acts_send.at[i], acts_recv.at[i], along_y[i]) for i in range(3)]
    for copy in acts_out:
        copy.start()
    acts_pair = [remote(own, own, pair_send.at[0], pair_recv.at[0], partner)]
    acts_pair[0].start()
    load_grads.wait()
    for part in range(ROUNDS):
        for xd in range(SIDE):
            start = xd * BLK + part * PART
            turned[part, xd * PART : (xd + 1) * PART, :] = grads[:, start : start + PART].T
    for i, s in enumerate((-1, 1, 2)):
        acts_out[i].wait_recv()
        here = acts.at[core, ring(y, s)]
        copy = remote(here, here, pair_send.at[i + 1], pair_recv.at[i + 1], partner)
        copy.start()
        acts_pair.append(copy)

    def halves(ref):
        return ref

    stages1, stages2, outs, crosses = {}, {}, {}, {}

    def which(r):
        return lax.rem(core + r // 2, 2), r % 2

    def products(r):
        h, v = which(r)
        if r == 2:
            for copy in acts_pair:
                copy.wait_recv()
        for u in range(2):
            left = turned[v * 2 + u]

            def step(zd, carry, u=u, left=left):
                value = jnp.dot(left, acts[h, zd], preferred_element_type=F32).astype(BF16)
                for xd in range(SIDE):
                    piece = value[xd * PART : (xd + 1) * PART]
                    if u == 0:
                        parts[r, 0, xd, zd // 2, lax.rem(zd, 2)] = piece
                    else:
                        parts[r, 1, zd, xd // 2, xd % 2] = piece
                return carry

            lax.fori_loop(0, SIDE, step, 0)
            me, (right, left_to) = ((x, along_x), (z, along_z))[u]
            stage = RingSum(
                lambda d, u=u: parts.at[r, u, d], me, right, left_to,
                far1.at[r, u], near1.at[r, u], send1.at[r, u], recv1.at[r, u],
            )
            stage.first()
            stages1[r, u] = stage

    def merge1(r):
        for u in range(2):
            stages1[r, u].merge()

    def between(r):
        for u in range(2):
            total = stages1[r, u].total()
            for half in range(2):
                for o in range(2):
                    for piece in range(2):
                        sums[r, u, half * 2 + o, piece] = total[half][o, piece * (PART // 2) : (piece + 1) * (PART // 2)]
            me, (right, left_to) = ((z, along_z), (x, along_x))[u]
            stage = RingSum(
                lambda d, u=u: sums.at[r, u, d], me, right, left_to,
                far2.at[r, u], near2.at[r, u], send2.at[r, u], recv2.at[r, u],
            )
            stage.first()
            stages2[r, u] = stage

    def merge2(r):
        for u in range(2):
            stages2[r, u].merge()

    def spread(r):
        h, v = which(r)
        for u in range(2):
            total = stages2[r, u].total()
            for half in range(2):
                start = u * PART + half * (PART // 2)
                done[r, start : start + PART // 2] = total[half]
        rows = pl.ds(v * 2 * PART, 2 * PART)
        there = all_ref.at[2 * group + h, rows]
        keep = pltpu.make_async_copy(done.at[r], there, local_sem.at[2 + r])
        keep.start()
        outs[r] = [remote(done.at[r], there, out_send.at[r, i], out_recv.at[r, i], along_y[i]) for i in range(3)]
        for copy in outs[r]:
            copy.start()
        cross = remote(done.at[r], there, cross_send.at[r, 0], cross_recv.at[r, 0], partner)
        cross.start()
        crosses[r] = [cross]
        outs[r, "keep"] = keep

    def pass_on(r):
        h, v = which(r)
        rows = pl.ds(v * 2 * PART, 2 * PART)
        for i, s in enumerate((-1, 1, 2)):
            outs[r][i].wait_recv()
            here = all_ref.at[2 * (2 * ring(y, s) + core) + h, rows]
            cross = remote(here, here, cross_send.at[r, i + 1], cross_recv.at[r, i + 1], partner)
            cross.start()
            crosses[r].append(cross)

    for step in range(ROUNDS + 4):
        if step < ROUNDS:
            products(step)
        if 0 <= step - 2 < ROUNDS:
            spread(step - 2)
        if 0 <= step - 1 < ROUNDS:
            between(step - 1)
        if 0 <= step < ROUNDS:
            merge1(step)
        if 0 <= step - 1 < ROUNDS:
            merge2(step - 1)
        if 0 <= step - 3 < ROUNDS:
            pass_on(step - 3)

    for copy in acts_out + acts_pair:
        copy.wait_send()
    for r in range(ROUNDS):
        for u in range(2):
            stages1[r, u].finish()
            stages2[r, u].finish()
        for copy in outs[r]:
            copy.wait_send()
        outs[r, "keep"].wait()
        for copy in crosses[r]:
            copy.wait()


def reduce_blocks(acts, grads):
    dma = pltpu.SemaphoreType.DMA
    return pl.pallas_call(
        reduce_kernel,
        out_shape=jax.ShapeDtypeStruct((16, BLK, BLK), BF16),
        in_specs=[pl.BlockSpec(memory_space=pl.ANY)] * 2,
        out_specs=pl.BlockSpec(memory_space=pl.ANY),
        scratch_shapes=[
            pltpu.VMEM((BLK, 4 * BLK), BF16),
            pltpu.VMEM((ROUNDS, BLK, BLK), BF16),
            pltpu.VMEM((2, SIDE, BLK, BLK), BF16),
            pltpu.VMEM((ROUNDS, 2, SIDE, 2, 2, PART, BLK), BF16),
            pltpu.VMEM((ROUNDS, 2, 2, 2, PART, BLK), BF16),
            pltpu.VMEM((ROUNDS, 2, 2, 2, 2, PART, BLK), BF16),
            pltpu.VMEM((ROUNDS, 2, SIDE, 2, PART // 2, BLK), BF16),
            pltpu.VMEM((ROUNDS, 2, 2, PART // 2, BLK), BF16),
            pltpu.VMEM((ROUNDS, 2, 2, 2, PART // 2, BLK), BF16),
            pltpu.VMEM((ROUNDS, 2 * PART, BLK), BF16),
            dma((2 + ROUNDS,)),
            dma((3,)), dma((3,)), dma((4,)), dma((4,)),
            dma((ROUNDS, 2, 6)), dma((ROUNDS, 2, 6)),
            dma((ROUNDS, 2, 6)), dma((ROUNDS, 2, 6)),
            dma((ROUNDS, 3)), dma((ROUNDS, 3)),
            dma((ROUNDS, 4)), dma((ROUNDS, 4)),
        ],
        compiler_params=pltpu.CompilerParams(
            collective_id=0, has_side_effects=True, vmem_limit_bytes=60 << 20
        ),
        cost_estimate=pl.CostEstimate(flops=2 * 512 * 2048 * 4096, bytes_accessed=12 << 20, transcendentals=0),
        name="reduce_blocks",
    )(acts, grads)


def slot_kernel(index_ref, used_ref, block_ref, ls_ref, rs_ref, lr_ref, rr_ref, ln_ref, rn_ref, out_ref):
    used = used_ref[pl.program_id(0)]
    owned = jnp.where(used > 0, block_ref[0], jnp.zeros_like(block_ref[0]))
    shaped = jnp.dot(lr_ref[0, 0, 0], owned, preferred_element_type=F32).astype(BF16)
    product = jnp.dot(shaped, rr_ref[0, 0, 0], preferred_element_type=F32)
    scaling = lax.rsqrt(jnp.mean(product * product) + EPSILON)
    out_ref[0] = (product * scaling).astype(BF16)
    left = lax.dot_general(owned, owned, (((1,), (1,)), ((), ())), preferred_element_type=F32)
    ln_ref[0, 0, 0] = STAT_DECAY * ls_ref[0, 0, 0] + (1.0 - STAT_DECAY) * left
    right = lax.dot_general(owned, owned, (((0,), (0,)), ((), ())), preferred_element_type=F32)
    rn_ref[0, 0, 0] = STAT_DECAY * rs_ref[0, 0, 0] + (1.0 - STAT_DECAY) * right


def slots_step(index, used, blocks, left_stats, right_stats, left_root, right_root):
    capacity = left_stats.shape[2]
    whole = pl.BlockSpec((1, 1, 1, BLK, BLK), lambda s, index, used: (0, 0, s, 0, 0))
    return pl.pallas_call(
        slot_kernel,
        grid_spec=pltpu.PrefetchScalarGridSpec(
            num_scalar_prefetch=2,
            grid=(capacity,),
            in_specs=[pl.BlockSpec((1, BLK, BLK), lambda s, index, used: (index[s], 0, 0))] + [whole] * 4,
            out_specs=[whole, whole, pl.BlockSpec((1, BLK, BLK), lambda s, index, used: (s, 0, 0))],
        ),
        out_shape=[
            jax.ShapeDtypeStruct(left_stats.shape, F32),
            jax.ShapeDtypeStruct(right_stats.shape, F32),
            jax.ShapeDtypeStruct((capacity, BLK, BLK), BF16),
        ],
        compiler_params=pltpu.CompilerParams(vmem_limit_bytes=40 << 20),
        name="slots_step",
    )(index, used, blocks, left_stats, right_stats, left_root, right_root)


def return_kernel(owner_ref, slot_ref, slots_ref, out_ref, held, packed, far, near, pair_send, pair_recv, send, recv):
    x, y, z, core = place()
    partner = device(x, y, z, 1 - core)
    right, left = [device(x, ring(y, s), z, core) for s in (1, -1)]
    greet([partner, right, left])
    swap = remote(slots_ref, held, pair_send.at[0], pair_recv.at[0], partner)
    swap.start()

    def block(step, h):
        k = 2 * (2 * ring(y, step) + core) + h
        return owner_ref[k], slot_ref[k]

    def mine(step, h, half):
        owner, slot = block(step, h)
        rows = pl.ds(half * (BLK // 2), BLK // 2)
        return jnp.where(lax.rem(owner, 2) == core, slots_ref[slot, rows], held[slot, rows])

    copies = []
    order = ((2, 0, 2, 1), (1, 1, -1, 0), (1, 0, -1, 1))
    landing = ((far.at[0], far.at[1]), (near.at[0, 1], near.at[1, 0]), (near.at[0, 0], near.at[1, 1]))
    for i in range(3):
        for j, target in enumerate((right, left)):
            copies.append(remote(packed.at[i, j], landing[i][j], send.at[2 * i + j], recv.at[2 * i + j], target))
    swap.wait_recv()
    for i in range(2):
        for j in range(2):
            step, half = order[i][2 * j], order[i][2 * j + 1]
            for h in range(2):
                packed[i, j, h] = mine(step, h, half)
            copies[2 * i + j].start()
    for j in range(2):
        step, half = order[2][2 * j], order[2][2 * j + 1]
        copies[j].wait_recv()
        for h in range(2):
            owner, _ = block(step, h)
            packed[2, j, h] = jnp.where(owner // 2 == y, mine(step, h, half), far[j, h])
        copies[4 + j].start()
    for h in range(2):
        for half in range(2):
            out_ref[h, half * (BLK // 2) : (half + 1) * (BLK // 2)] = mine(0, h, half)
    for copy in copies[2:]:
        copy.wait_recv()
    for h in range(2):
        owner, _ = block(0, h)
        for half in range(2):
            rows = slice(half * (BLK // 2), (half + 1) * (BLK // 2))
            from_left = (owner // 2 == ring(y, -1)) | ((owner // 2 == ring(y, 2)) & (half == 0))
            value = jnp.where(from_left, near[0, half, h], near[1, half, h])
            out_ref[h, rows] = jnp.where(owner // 2 == y, out_ref[h, rows], value)
    swap.wait_send()
    for copy in copies:
        copy.wait_send()


def return_blocks(owner, slot, slots):
    dma = pltpu.SemaphoreType.DMA
    half = (2, BLK // 2, BLK)
    return pl.pallas_call(
        return_kernel,
        out_shape=jax.ShapeDtypeStruct((2, BLK, BLK), BF16),
        in_specs=[pl.BlockSpec(memory_space=pltpu.SMEM)] * 2 + [pl.BlockSpec(memory_space=pltpu.VMEM)],
        out_specs=pl.BlockSpec(memory_space=pltpu.VMEM),
        scratch_shapes=[
            pltpu.VMEM(slots.shape, BF16),
            pltpu.VMEM((3, 2) + half, BF16),
            pltpu.VMEM((2,) + half, BF16),
            pltpu.VMEM((2, 2) + half, BF16),
            dma((1,)), dma((1,)), dma((6,)), dma((6,)),
        ],
        compiler_params=pltpu.CompilerParams(
            collective_id=1, has_side_effects=True, vmem_limit_bytes=40 << 20
        ),
        cost_estimate=pl.CostEstimate(flops=0, bytes_accessed=8 << 20, transcendentals=0),
        name="return_blocks",
    )(owner, slot, slots)


def body(acts, grads_out, owners, left_stats, right_stats, left_root, right_root):
    capacity = left_stats.shape[2]
    my_index = lax.axis_index("group")
    owner = owners[0, :, 0]
    position = jnp.arange(owner.shape[0], dtype=jnp.int32)
    matches = owner[:, None] == owner[None, :]
    earlier = position[None, :] < position[:, None]
    slot = jnp.sum((matches & earlier).astype(jnp.int32), axis=1)
    here = (owner[None, :] == my_index) & (slot[None, :] == jnp.arange(capacity, dtype=jnp.int32)[:, None])
    index = jnp.sum(jnp.where(here, position[None, :], 0), axis=1)
    used = jnp.sum(here.astype(jnp.int32), axis=1)

    blocks = reduce_blocks(acts, grads_out)
    left_new, right_new, slots = slots_step(index, used, blocks, left_stats, right_stats, left_root, right_root)
    update = return_blocks(owner, slot, slots)
    return (left_new, right_new, update)


def solution(mesh):
    placed = (
        P("dp", "group"),
        P("dp", "group"),
        P("dp", None, None),
        P("dp", "group", None, None, None),
        P("dp", "group", None, None, None),
        P("dp", "group", None, None, None),
        P("dp", "group", None, None, None),
    )
    return jax.shard_map(
        body,
        mesh=mesh,
        in_specs=placed,
        out_specs=(
            P("dp", "group", None, None, None),
            P("dp", "group", None, None, None),
            P(("group", "dp"), None, None),
        ),
        check_vma=False,
    )
```

```python
import functools

import jax
import jax.numpy as jnp
from jax import lax
from jax.experimental import pallas as pl
from jax.experimental.pallas import tpu as pltpu
from jax.sharding import PartitionSpec as P

MESH = pl.DeviceIdType.MESH
STAT_DECAY = 0.9
EPSILON = 1e-06
BLK = 512
HALF = BLK // 2
SIDE = 4
GROUPS = 8
CAP = 3
PER_HALF = 4
ROUNDS = 2 * PER_HALF
PART = HALF // PER_HALF
SLOTS = 3
F32 = jnp.float32
BF16 = jnp.bfloat16


def place():
    dp, group = lax.axis_index("dp"), lax.axis_index("group")
    return dp // SIDE, group // 2, lax.rem(dp, SIDE), lax.rem(group, 2)


def ring(index, step):
    return lax.rem(index + step + SIDE, SIDE)


def device(x, y, z, core):
    return (x * SIDE + z, y * 2 + core)


def remote(src, dst, send, recv, target):
    return pltpu.make_async_remote_copy(
        src_ref=src, dst_ref=dst, send_sem=send, recv_sem=recv, device_id=target, device_id_type=MESH
    )


def greet(targets):
    barrier = pltpu.get_barrier_semaphore()
    for target in targets:
        pl.semaphore_signal(barrier, inc=1, device_id=target, device_id_type=MESH)
    pl.semaphore_wait(barrier, len(targets))


def plus(*terms):
    total = terms[0].astype(F32)
    for term in terms[1:]:
        total = total + term.astype(F32)
    return total.astype(BF16)


class RingSum:
    def __init__(self, part, me, right, left, far, near, send, recv):
        self.part, self.me = part, me
        to_right = [
            (part(ring(me, 2)).at[0], far.at[0]),
            (part(ring(me, 1)).at[1], near.at[0, 1]),
            (part(ring(me, 1)).at[0], near.at[0, 0]),
        ]
        to_left = [
            (part(ring(me, 2)).at[1], far.at[1]),
            (part(ring(me, -1)).at[0], near.at[1, 0]),
            (part(ring(me, -1)).at[1], near.at[1, 1]),
        ]
        self.far, self.near = far, near
        self.copies = []
        for i in range(3):
            for j, (target, lists) in enumerate(((right, to_right), (left, to_left))):
                src, dst = lists[i]
                self.copies.append(remote(src, dst, send.at[2 * i + j], recv.at[2 * i + j], target))

    def first(self):
        for copy in self.copies[:4]:
            copy.start()

    def merge(self):
        for j, (step, half) in enumerate(((1, 0), (-1, 1))):
            self.copies[j].wait_recv()
            ref = self.part(ring(self.me, step)).at[half]
            ref[...] = plus(ref[...], self.far[j])
            self.copies[4 + j].start()

    def total(self):
        for copy in self.copies[2:]:
            copy.wait_recv()
        mine = self.part(self.me)
        return [plus(mine[half], self.near[0, half], self.near[1, half]) for half in range(2)]

    def finish(self):
        for copy in self.copies:
            copy.wait_send()


def shampoo_kernel(
    table, acts_ref, grads_ref, ls_ref, rs_ref, lr_ref, rr_ref,
    ln_ref, rn_ref, out_ref,
    grads, turned, acts, parts, far1, near1, sums, far2, near2, blocks0, blocks1,
    left_root, right_root, result0, result1, held0, held1, packed, back_far, back_near, left_stats, right_stats,
    local_sem, acts_send, acts_recv, pair_send, pair_recv,
    send1, recv1, send2, recv2, out_send, out_recv, cross_send, cross_recv,
    swap_send, swap_recv, back_send, back_recv, stats_sem,
):
    x, y, z, core = place()
    group = y * 2 + core
    partner = device(x, y, z, 1 - core)
    along_y = [device(x, ring(y, s), z, core) for s in (1, -1, 2)]
    along_x = [device(ring(x, s), y, z, core) for s in (1, -1)]
    along_z = [device(x, y, ring(z, s), core) for s in (1, -1)]
    blocks, result, held = (blocks0, blocks1), (result0, result1), (held0, held1)

    load_grads = pltpu.make_async_copy(grads_ref, grads, local_sem.at[0])
    load_acts = pltpu.make_async_copy(acts_ref, acts.at[core, y], local_sem.at[1])
    load_acts.start()
    load_grads.start()
    loads = [
        pltpu.make_async_copy(ref.at[0, 0], buffer, local_sem.at[2 + i])
        for i, (ref, buffer) in enumerate(
            ((lr_ref, left_root), (rr_ref, right_root), (ls_ref, left_stats), (rs_ref, right_stats))
        )
    ]
    greet([partner] + along_y + along_x + along_z)

    load_acts.wait()
    own = acts.at[core, y]
    acts_out = [remote(own, own, acts_send.at[i], acts_recv.at[i], along_y[i]) for i in range(3)]
    for copy in acts_out:
        copy.start()
    acts_pair = [remote(own, own, pair_send.at[0], pair_recv.at[0], partner)]
    acts_pair[0].start()
    load_grads.wait()
    for copy in loads:
        copy.start()
    for part in range(HALF // PART * 2):
        for xd in range(SIDE):
            start = xd * BLK + part * PART
            turned[part, xd * PART : (xd + 1) * PART, :] = grads[:, start : start + PART].T
    for i, s in enumerate((-1, 1, 2)):
        acts_out[i].wait_recv()
        here = acts.at[core, ring(y, s)]
        copy = remote(here, here, pair_send.at[i + 1], pair_recv.at[i + 1], partner)
        copy.start()
        acts_pair.append(copy)

    stages1, stages2, outs, crosses = {}, {}, {}, {}

    def products(r):
        p, v = r // PER_HALF, r % PER_HALF
        h, b = lax.rem(core + p, 2), r % SLOTS
        if r == PER_HALF:
            for copy in acts_pair:
                copy.wait_recv()
        for u in range(2):
            if r >= SLOTS:
                stages1[r - SLOTS, u].finish()
            left = turned[v * 2 + u]

            def step(zd, carry, u=u, left=left):
                value = jnp.dot(left, acts[h, zd], preferred_element_type=F32).astype(BF16)
                for xd in range(SIDE):
                    piece = value[xd * PART : (xd + 1) * PART]
                    if u == 0:
                        parts[b, 0, xd, zd // 2, lax.rem(zd, 2)] = piece
                    else:
                        parts[b, 1, zd, xd // 2, xd % 2] = piece
                return carry

            lax.fori_loop(0, SIDE, step, 0)
            me, (right, left_to) = ((x, along_x), (z, along_z))[u]
            stage = RingSum(
                lambda d, u=u: parts.at[b, u, d], me, right, left_to,
                far1.at[b, u], near1.at[b, u], send1.at[b, u], recv1.at[b, u],
            )
            stage.first()
            stages1[r, u] = stage

    def merge1(r):
        for u in range(2):
            stages1[r, u].merge()

    def between(r):
        b = r % SLOTS
        for u in range(2):
            if r >= SLOTS:
                stages2[r - SLOTS, u].finish()
            total = stages1[r, u].total()
            for half in range(2):
                for o in range(2):
                    for piece in range(2):
                        sums[b, u, half * 2 + o, piece] = total[half][o, piece * (PART // 2) : (piece + 1) * (PART // 2)]
            me, (right, left_to) = ((z, along_z), (x, along_x))[u]
            stage = RingSum(
                lambda d, u=u: sums.at[b, u, d], me, right, left_to,
                far2.at[b, u], near2.at[b, u], send2.at[b, u], recv2.at[b, u],
            )
            stage.first()
            stages2[r, u] = stage

    def merge2(r):
        for u in range(2):
            stages2[r, u].merge()

    def spread(r):
        p, v = r // PER_HALF, r % PER_HALF
        for u in range(2):
            total = stages2[r, u].total()
            for half in range(2):
                start = (2 * v + u) * PART + half * (PART // 2)
                blocks[p][group, start : start + PART // 2] = total[half]
        here = blocks[p].at[group, pl.ds(v * 2 * PART, 2 * PART)]
        outs[r] = [remote(here, here, out_send.at[r, i], out_recv.at[r, i], along_y[i]) for i in range(3)]
        for copy in outs[r]:
            copy.start()
        cross = remote(here, here, cross_send.at[r, 0], cross_recv.at[r, 0], partner)
        cross.start()
        crosses[r] = [cross]

    def pass_on(r):
        p, v = r // PER_HALF, r % PER_HALF
        for i, s in enumerate((-1, 1, 2)):
            outs[r][i].wait_recv()
            here = blocks[p].at[2 * ring(y, s) + core, pl.ds(v * 2 * PART, 2 * PART)]
            cross = remote(here, here, cross_send.at[r, i + 1], cross_recv.at[r, i + 1], partner)
            cross.start()
            crosses[r].append(cross)

    swaps, backs = {}, {}

    def precondition(p):
        for r in range(p * PER_HALF, (p + 1) * PER_HALF):
            for copy in crosses[r]:
                copy.wait_recv()
        if p == 0:
            for copy in loads:
                copy.wait()
        swaps[p] = []
        for j in range(CAP):
            block = blocks[p][table[32 + 6 * p + 2 * j]]
            slot = table[33 + 6 * p + 2 * j]
            shaped = jnp.dot(left_root[slot], block, preferred_element_type=F32).astype(BF16)
            product = jnp.dot(shaped, right_root[slot], preferred_element_type=F32)
            scaling = lax.rsqrt(jnp.mean(product * product) + EPSILON)
            result[p][j] = (product * scaling).astype(BF16)
            copy = remote(result[p].at[j], held[p].at[j], swap_send.at[p, j], swap_recv.at[p, j], partner)
            copy.start()
            swaps[p].append(copy)

    def mine(p, step, half):
        to = 2 * ring(y, step) + core
        owner, rank = table[16 * p + to], table[16 * p + 8 + to]
        rows = pl.ds(half * HALF, HALF)
        value = jnp.where(lax.rem(owner, 2) == core, result[p][rank, rows], held[p][rank, rows])
        return value, owner // 2

    order = (((2, 0), (2, 1)), ((1, 1), (-1, 0)), ((1, 0), (-1, 1)))

    def back_first(p):
        for copy in swaps[p]:
            copy.wait_recv()
        far, near = back_far.at[p], back_near.at[p]
        landing = ((far.at[0], far.at[1]), (near.at[0, 1], near.at[1, 0]), (near.at[0, 0], near.at[1, 1]))
        backs[p] = []
        for i in range(3):
            for j in range(2):
                backs[p].append(
                    remote(
                        packed.at[p, i, j], landing[i][j], back_send.at[p, 2 * i + j], back_recv.at[p, 2 * i + j], along_y[j]
                    )
                )
        for i in range(2):
            for j in range(2):
                packed[p, i, j] = mine(p, *order[i][j])[0]
                backs[p][2 * i + j].start()

    def back_merge(p):
        for j in range(2):
            backs[p][j].wait_recv()
            value, at = mine(p, *order[2][j])
            packed[p, 2, j] = jnp.where(at == y, value, back_far[p, j])
            backs[p][4 + j].start()

    def back_last(p):
        for copy in backs[p][2:]:
            copy.wait_recv()
        h = lax.rem(core + p, 2)
        for half in range(2):
            value, at = mine(p, 0, half)
            from_left = at == ring(y, -1)
            if half == 0:
                from_left = from_left | (at == ring(y, 2))
            value = jnp.where(at == y, value, jnp.where(from_left, back_near[p, 0, half], back_near[p, 1, half]))
            out_ref[h, half * HALF : (half + 1) * HALF] = value

    stats_out = []

    def grams(s):
        p, at, used = table[44 + 3 * s], table[45 + 3 * s], table[46 + 3 * s]
        block = jnp.where(p == 0, blocks0[at], blocks1[at])
        block = jnp.where(used > 0, block, jnp.zeros_like(block))
        left = lax.dot_general(block, block, (((1,), (1,)), ((), ())), preferred_element_type=F32)
        left_stats[s] = STAT_DECAY * left_stats[s] + (1.0 - STAT_DECAY) * left
        right = lax.dot_general(block, block, (((0,), (0,)), ((), ())), preferred_element_type=F32)
        right_stats[s] = STAT_DECAY * right_stats[s] + (1.0 - STAT_DECAY) * right
        for i, (buffer, ref) in enumerate(((left_stats, ln_ref), (right_stats, rn_ref))):
            copy = pltpu.make_async_copy(buffer.at[s], ref.at[0, 0, s], stats_sem.at[2 * s + i])
            copy.start()
            stats_out.append(copy)

    for step in range(ROUNDS + 2):
        if step < ROUNDS:
            products(step)
        if 0 <= step - 2 < ROUNDS:
            spread(step - 2)
        if 0 <= step - 1 < ROUNDS:
            between(step - 1)
        if step == PER_HALF + 2:
            precondition(0)
        if 0 <= step < ROUNDS:
            merge1(step)
        if 0 <= step - 1 < ROUNDS:
            merge2(step - 1)
        if 0 <= step - 2 < ROUNDS:
            pass_on(step - 2)
        if step == PER_HALF + 2:
            back_first(0)
        if step == PER_HALF + 3:
            back_merge(0)
    precondition(1)
    back_first(1)
    grams(0)
    grams(1)
    back_merge(1)
    grams(2)
    back_last(0)
    back_last(1)

    for copy in acts_out + acts_pair:
        copy.wait_send()
    for r in range(ROUNDS):
        if r >= ROUNDS - SLOTS:
            for u in range(2):
                stages1[r, u].finish()
                stages2[r, u].finish()
        for copy in outs[r] + crosses[r]:
            copy.wait_send()
    for p in range(2):
        for copy in swaps[p] + backs[p]:
            copy.wait_send()
    for copy in stats_out:
        copy.wait()


def body(acts, grads_out, owners, left_stats, right_stats, left_root, right_root):
    my_index = lax.axis_index("group")
    owner = owners[0, :, 0]
    position = jnp.arange(owner.shape[0], dtype=jnp.int32)
    half = (position // 2 + position) % 2
    matches = owner[:, None] == owner[None, :]
    earlier = matches & (position[None, :] < position[:, None])
    slot = jnp.sum(earlier.astype(jnp.int32), axis=1)
    rank = jnp.sum((earlier & (half[:, None] == half[None, :])).astype(jnp.int32), axis=1)
    count = jnp.arange(CAP, dtype=jnp.int32)
    entries = []
    for p in range(2):
        at = 2 * jnp.arange(GROUPS, dtype=jnp.int32) + (jnp.arange(GROUPS, dtype=jnp.int32) + p) % 2
        entries += [owner[at], rank[at]]
    for p in range(2):
        here = (owner == my_index)[None, :] & (half == p)[None, :] & (rank[None, :] == count[:, None])
        which = jnp.sum(jnp.where(here, position[None, :] // 2, 0), axis=1)
        where = jnp.sum(jnp.where(here, slot[None, :], 0), axis=1)
        entries.append(jnp.stack([which, where], axis=1).reshape(-1))
    here = (owner == my_index)[None, :] & (slot[None, :] == count[:, None])
    entries.append(
        jnp.stack(
            [
                jnp.sum(jnp.where(here, half[None, :], 0), axis=1),
                jnp.sum(jnp.where(here, position[None, :] // 2, 0), axis=1),
                jnp.sum(here.astype(jnp.int32), axis=1),
            ],
            axis=1,
        ).reshape(-1)
    )
    table = jnp.concatenate(entries)

    dma = pltpu.SemaphoreType.DMA
    piece, small = (2, PART, BLK), (PART // 2, BLK)
    square = (BLK, BLK)
    left_new, right_new, update = pl.pallas_call(
        shampoo_kernel,
        out_shape=(
            jax.ShapeDtypeStruct(left_stats.shape, F32),
            jax.ShapeDtypeStruct(right_stats.shape, F32),
            jax.ShapeDtypeStruct((2, BLK, BLK), BF16),
        ),
        in_specs=[pl.BlockSpec(memory_space=pltpu.SMEM)] + [pl.BlockSpec(memory_space=pl.ANY)] * 6,
        out_specs=(
            pl.BlockSpec(memory_space=pl.ANY),
            pl.BlockSpec(memory_space=pl.ANY),
            pl.BlockSpec(memory_space=pltpu.VMEM),
        ),
        scratch_shapes=[
            pltpu.VMEM((BLK, SIDE * BLK), BF16),
            pltpu.VMEM((2 * PER_HALF, SIDE * PART, BLK), BF16),
            pltpu.VMEM((2, SIDE) + square, BF16),
            pltpu.VMEM((SLOTS, 2, SIDE, 2) + piece, BF16),
            pltpu.VMEM((SLOTS, 2, 2) + piece, BF16),
            pltpu.VMEM((SLOTS, 2, 2, 2) + piece, BF16),
            pltpu.VMEM((SLOTS, 2, SIDE, 2) + small, BF16),
            pltpu.VMEM((SLOTS, 2, 2) + small, BF16),
            pltpu.VMEM((SLOTS, 2, 2, 2) + small, BF16),
            pltpu.VMEM((GROUPS,) + square, BF16),
            pltpu.VMEM((GROUPS,) + square, BF16),
            pltpu.VMEM((CAP,) + square, BF16),
            pltpu.VMEM((CAP,) + square, BF16),
            pltpu.VMEM((CAP,) + square, BF16),
            pltpu.VMEM((CAP,) + square, BF16),
            pltpu.VMEM((CAP,) + square, BF16),
            pltpu.VMEM((CAP,) + square, BF16),
            pltpu.VMEM((2, 3, 2, HALF, BLK), BF16),
            pltpu.VMEM((2, 2, HALF, BLK), BF16),
            pltpu.VMEM((2, 2, 2, HALF, BLK), BF16),
            pltpu.VMEM((CAP,) + square, F32),
            pltpu.VMEM((CAP,) + square, F32),
            dma((6,)),
            dma((3,)), dma((3,)), dma((4,)), dma((4,)),
            dma((SLOTS, 2, 6)), dma((SLOTS, 2, 6)),
            dma((SLOTS, 2, 6)), dma((SLOTS, 2, 6)),
            dma((ROUNDS, 3)), dma((ROUNDS, 3)),
            dma((ROUNDS, 4)), dma((ROUNDS, 4)),
            dma((2, CAP)), dma((2, CAP)),
            dma((2, 6)), dma((2, 6)),
            dma((2 * CAP,)),
        ],
        compiler_params=pltpu.CompilerParams(
            collective_id=0, has_side_effects=True, vmem_limit_bytes=62 << 20
        ),
        cost_estimate=pl.CostEstimate(flops=12 << 30, bytes_accessed=20 << 20, transcendentals=0),
        name="shampoo",
    )(table, acts, grads_out, left_stats, right_stats, left_root, right_root)
    return (left_new, right_new, update)


def solution(mesh):
    placed = (
        P("dp", "group"),
        P("dp", "group"),
        P("dp", None, None),
        P("dp", "group", None, None, None),
        P("dp", "group", None, None, None),
        P("dp", "group", None, None, None),
        P("dp", "group", None, None, None),
    )
    return jax.shard_map(
        body,
        mesh=mesh,
        in_specs=placed,
        out_specs=(
            P("dp", "group", None, None, None),
            P("dp", "group", None, None, None),
            P(("group", "dp"), None, None),
        ),
        check_vma=False,
    )
```

```python
import functools

import jax
import jax.numpy as jnp
from jax import lax
from jax.experimental import pallas as pl
from jax.experimental.pallas import tpu as pltpu
from jax.sharding import PartitionSpec as P

MESH = pl.DeviceIdType.MESH
STAT_DECAY = 0.9
EPSILON = 1e-06
BLK = 512
HALF = BLK // 2
SIDE = 4
GROUPS = 8
CAP = 3
PER_HALF = 4
ROUNDS = 2 * PER_HALF
PART = HALF // PER_HALF
SLOTS = 3
F32 = jnp.float32
BF16 = jnp.bfloat16


def place():
    dp, group = lax.axis_index("dp"), lax.axis_index("group")
    return dp // SIDE, group // 2, lax.rem(dp, SIDE), lax.rem(group, 2)


def ring(index, step):
    return lax.rem(index + step + SIDE, SIDE)


def device(x, y, z, core):
    return (x * SIDE + z, y * 2 + core)


def remote(src, dst, send, recv, target):
    return pltpu.make_async_remote_copy(
        src_ref=src, dst_ref=dst, send_sem=send, recv_sem=recv, device_id=target, device_id_type=MESH
    )


def greet(targets):
    barrier = pltpu.get_barrier_semaphore()
    for target in targets:
        pl.semaphore_signal(barrier, inc=1, device_id=target, device_id_type=MESH)
    pl.semaphore_wait(barrier, len(targets))


def plus(*terms):
    total = terms[0].astype(F32)
    for term in terms[1:]:
        total = total + term.astype(F32)
    return total.astype(BF16)


class RingSum:
    def __init__(self, part, me, right, left, far, near, send, recv):
        self.part, self.me = part, me
        to_right = [
            (part(ring(me, 2)).at[0], far.at[0]),
            (part(ring(me, 1)).at[1], near.at[0, 1]),
            (part(ring(me, 1)).at[0], near.at[0, 0]),
        ]
        to_left = [
            (part(ring(me, 2)).at[1], far.at[1]),
            (part(ring(me, -1)).at[0], near.at[1, 0]),
            (part(ring(me, -1)).at[1], near.at[1, 1]),
        ]
        self.far, self.near = far, near
        self.copies = []
        for i in range(3):
            for j, (target, lists) in enumerate(((right, to_right), (left, to_left))):
                src, dst = lists[i]
                self.copies.append(remote(src, dst, send.at[2 * i + j], recv.at[2 * i + j], target))

    def first(self):
        for copy in self.copies[:4]:
            copy.start()

    def merge(self):
        for j, (step, half) in enumerate(((1, 0), (-1, 1))):
            self.copies[j].wait_recv()
            ref = self.part(ring(self.me, step)).at[half]
            ref[...] = plus(ref[...], self.far[j])
            self.copies[4 + j].start()

    def total(self):
        for copy in self.copies[2:]:
            copy.wait_recv()
        mine = self.part(self.me)
        return [plus(mine[half], self.near[0, half], self.near[1, half]) for half in range(2)]

    def finish(self):
        for copy in self.copies:
            copy.wait_send()


def gradient_kernel(
    owners, acts_ref, grads_ref, lr_ref, rr_ref,
    owned_ref, out_ref,
    grads, turned, acts, parts, far1, near1, sums, far2, near2, blocks0, blocks1,
    roots, pair_roots, roots_packed, roots_far, roots_near, holder_roots,
    result, held, packed, back_far, back_near, owned, slot_table, rank_table,
    local_sem, pair_send, pair_recv, acts_send, acts_recv, acts_cross_send, acts_cross_recv,
    send1, recv1, send2, recv2, out_send, out_recv, cross_send, cross_recv,
    swap_send, swap_recv, back_send, back_recv, roots_swap_send, roots_swap_recv, roots_send, roots_recv, owned_sem,
):
    x, y, z, core = place()
    group = y * 2 + core
    partner = device(x, y, z, 1 - core)
    along_y = [device(x, ring(y, s), z, core) for s in (1, -1)]
    along_x = [device(ring(x, s), y, z, core) for s in (1, -1)]
    along_z = [device(x, y, ring(z, s), core) for s in (1, -1)]
    blocks = (blocks0, blocks1)
    started = []

    def go(copy):
        copy.start()
        started.append(copy)
        return copy

    load_acts = pltpu.make_async_copy(acts_ref, acts.at[core, y], local_sem.at[0])
    load_grads = pltpu.make_async_copy(grads_ref, grads, local_sem.at[1])
    load_roots = [
        pltpu.make_async_copy(ref.at[0, 0], roots.at[i], local_sem.at[2 + i]) for i, ref in enumerate((lr_ref, rr_ref))
    ]
    load_acts.start()
    load_grads.start()
    for copy in load_roots:
        copy.start()
    greet([partner] + along_y + along_x + along_z)

    load_acts.wait()
    own = acts.at[core, y]
    pair = go(remote(own, own, pair_send.at[0], pair_recv.at[0], partner))
    gathers = {}

    def rows_of(h, at, start, size):
        return acts.at[h, at, pl.ds(pl.multiple_of(core * HALF + start, 16), size)]

    def acts_first(h):
        here = rows_of(h, y, 0, HALF)
        gathers[h] = [
            go(remote(here, here, acts_send.at[h, j], acts_recv.at[h, j], along_y[j])) for j in range(2)
        ]
        gathers[h, "cross"] = []

    def acts_cross(h, i, at):
        here = rows_of(h, at, 0, HALF)
        gathers[h, "cross"].append(
            go(remote(here, here, acts_cross_send.at[h, i], acts_cross_recv.at[h, i], partner))
        )

    def acts_forward(h):
        for j in range(2):
            gathers[h][j].wait_recv()
            at = ring(y, (-1, 1)[j])
            here = rows_of(h, at, j * (HALF // 2), HALF // 2)
            gathers[h].append(
                go(remote(here, here, acts_send.at[h, 2 + j], acts_recv.at[h, 2 + j], along_y[j]))
            )
            acts_cross(h, j, at)

    def acts_last(h):
        for copy in gathers[h][2:]:
            copy.wait_recv()
        acts_cross(h, 2, ring(y, 2))

    def acts_ready(h):
        for copy in gathers[h, "cross"]:
            copy.wait_recv()

    pair.wait_recv()
    acts_first(0)

    count = 2 * GROUPS
    owner = [owners[k] for k in range(count)]
    zero, one = jnp.int32(0), jnp.int32(1)
    slot, rank = [], []
    for k in range(count):
        same = [jnp.where(owner[k2] == owner[k], one, zero) for k2 in range(k)]
        slot.append(sum(same, zero))
        rank.append(sum(same[0::2], zero))
        slot_table[k] = jnp.minimum(slot[k], CAP - 1)
        rank_table[k] = jnp.minimum(rank[k], CAP - 1)
    is_mine = [owner[k] == group for k in range(count)]

    def pick(positions, test, value):
        return sum([jnp.where(is_mine[k] & test(k), value(k), zero) for k in positions], zero)

    load_grads.wait()
    for part in range(2 * PER_HALF):
        for xd in range(SIDE):
            start = xd * BLK + part * PART
            turned[part, xd * PART : (xd + 1) * PART, :] = grads[:, start : start + PART].T
    acts_forward(0)
    for copy in load_roots:
        copy.wait()
    acts_last(0)
    roots_swap = go(remote(roots, pair_roots, roots_swap_send.at[0], roots_swap_recv.at[0], partner))

    stages1, stages2, outs, crosses = {}, {}, {}, {}

    def products(r):
        p, v = r // PER_HALF, r % PER_HALF
        b = r % SLOTS
        if v == 0:
            acts_ready(p)
        for u in range(2):
            if r >= SLOTS:
                stages1[r - SLOTS, u].finish()
            left = turned[v * 2 + u]

            def step(zd, carry, u=u, left=left):
                value = jnp.dot(left, acts[p, zd], preferred_element_type=F32).astype(BF16)
                for xd in range(SIDE):
                    piece = value[xd * PART : (xd + 1) * PART]
                    if u == 0:
                        parts[b, 0, xd, zd // 2, lax.rem(zd, 2)] = piece
                    else:
                        parts[b, 1, zd, xd // 2, xd % 2] = piece
                return carry

            lax.fori_loop(0, SIDE, step, 0)
            me, (right, left_to) = ((x, along_x), (z, along_z))[u]
            stage = RingSum(
                lambda d, u=u: parts.at[b, u, d], me, right, left_to,
                far1.at[b, u], near1.at[b, u], send1.at[b, u], recv1.at[b, u],
            )
            stage.first()
            stages1[r, u] = stage

    def merge1(r):
        for u in range(2):
            stages1[r, u].merge()

    def between(r):
        b = r % SLOTS
        for u in range(2):
            if r >= SLOTS:
                stages2[r - SLOTS, u].finish()
            total = stages1[r, u].total()
            for half in range(2):
                for o in range(2):
                    for piece in range(2):
                        sums[b, u, half * 2 + o, piece] = total[half][o, piece * (PART // 2) : (piece + 1) * (PART // 2)]
            me, (right, left_to) = ((z, along_z), (x, along_x))[u]
            stage = RingSum(
                lambda d, u=u: sums.at[b, u, d], me, right, left_to,
                far2.at[b, u], near2.at[b, u], send2.at[b, u], recv2.at[b, u],
            )
            stage.first()
            stages2[r, u] = stage

    def merge2(r):
        for u in range(2):
            stages2[r, u].merge()

    def strip(r, at, start, size):
        return blocks[r // PER_HALF].at[at, pl.ds((r % PER_HALF) * 2 * PART + start, size)]

    def cross(r, i, at):
        here = strip(r, at, 0, 2 * PART)
        crosses[r].append(go(remote(here, here, cross_send.at[r, i], cross_recv.at[r, i], partner)))

    def spread(r):
        p, v = r // PER_HALF, r % PER_HALF
        for u in range(2):
            total = stages2[r, u].total()
            for half in range(2):
                start = (2 * v + u) * PART + half * (PART // 2)
                blocks[p][group, start : start + PART // 2] = total[half]
        here = strip(r, group, 0, 2 * PART)
        outs[r] = [go(remote(here, here, out_send.at[r, j], out_recv.at[r, j], along_y[j])) for j in range(2)]
        crosses[r] = []
        cross(r, 0, group)

    def pass_on(r):
        for j in range(2):
            outs[r][j].wait_recv()
            at = 2 * ring(y, (-1, 1)[j]) + core
            here = strip(r, at, j * PART, PART)
            outs[r].append(go(remote(here, here, out_send.at[r, 2 + j], out_recv.at[r, 2 + j], along_y[j])))
            cross(r, 1 + j, at)

    def pass_last(r):
        for copy in outs[r][2:]:
            copy.wait_recv()
        cross(r, 3, 2 * ring(y, 2) + core)

    def blocks_ready(p):
        for r in range(p * PER_HALF, (p + 1) * PER_HALF):
            for copy in crosses[r]:
                copy.wait_recv()

    def condition(left_root, block, right_root):
        shaped = jnp.dot(left_root, block, preferred_element_type=F32).astype(BF16)
        product = jnp.dot(shaped, right_root, preferred_element_type=F32)
        scaling = lax.rsqrt(jnp.mean(product * product) + EPSILON)
        return (product * scaling).astype(BF16)

    swaps = []

    def precondition():
        for j in range(CAP):
            def test(k, j=j):
                return rank[k] == j

            even = range(0, count, 2)
            which, at = pick(even, test, lambda k: jnp.int32(k // 2)), pick(even, test, lambda k: jnp.minimum(slot[k], CAP - 1))
            result[j] = condition(roots[0, at], blocks0[which], roots[1, at])
            swaps.append(go(remote(result.at[j], held.at[j], swap_send.at[j], swap_recv.at[j], partner)))

    class Routed:
        def __init__(self, parity, table, sources, packed, far, near, send, recv):
            self.parity, self.table, self.sources = parity, table, sources
            self.packed, self.far, self.near = packed, far, near
            self.order = (((2, 0), (2, 1)), ((1, 1), (-1, 0)), ((1, 0), (-1, 1)))
            landing = ((far.at[0], far.at[1]), (near.at[0, 1], near.at[1, 0]), (near.at[0, 0], near.at[1, 1]))
            self.copies = [
                remote(packed.at[i, j], landing[i][j], send.at[2 * i + j], recv.at[2 * i + j], along_y[j])
                for i in range(3)
                for j in range(2)
            ]

        def mine(self, step, half):
            k = 2 * (2 * ring(y, step) + core) + self.parity
            owner, at = owners[k], self.table[k]
            rows = pl.ds(half * HALF, HALF)
            return [
                jnp.where(lax.rem(owner, 2) == core, here(at, rows), there(at, rows)) for here, there in self.sources
            ], owner // 2

        def first(self):
            for i in range(2):
                for j in range(2):
                    for n, value in enumerate(self.mine(*self.order[i][j])[0]):
                        self.packed[i, j, n] = value
                    go(self.copies[2 * i + j])

        def merge(self):
            for j in range(2):
                self.copies[j].wait_recv()
                values, at = self.mine(*self.order[2][j])
                for n, value in enumerate(values):
                    self.packed[2, j, n] = jnp.where(at == y, value, self.far[j, n])
                go(self.copies[4 + j])

        def last(self, store):
            for copy in self.copies[2:]:
                copy.wait_recv()
            for half in range(2):
                values, at = self.mine(0, half)
                from_left = at == ring(y, -1)
                if half == 0:
                    from_left = from_left | (at == ring(y, 2))
                for n, value in enumerate(values):
                    arrived = jnp.where(from_left, self.near[0, half, n], self.near[1, half, n])
                    store(n, half, jnp.where(at == y, value, arrived))

    back = Routed(
        0, rank_table, [(lambda at, rows: result[at, rows], lambda at, rows: held[at, rows])],
        packed, back_far, back_near, back_send, back_recv,
    )
    routed = Routed(
        1, slot_table,
        [(lambda at, rows, n=n: roots[n, at, rows], lambda at, rows, n=n: pair_roots[n, at, rows]) for n in range(2)],
        roots_packed, roots_far, roots_near, roots_send, roots_recv,
    )

    def store_roots(n, half, value):
        holder_roots[n, half * HALF : (half + 1) * HALF] = value

    def store_update(n, half, value):
        out_ref[0, half * HALF : (half + 1) * HALF] = value

    def collect(s):
        def test(k):
            return slot[k] == s

        every = range(count)
        odd = pick(every, test, lambda k: jnp.int32(k % 2))
        at = pick(every, test, lambda k: jnp.int32(k // 2))
        used = pick(every, test, lambda k: one)
        block = jnp.where(odd > 0, blocks1[at], blocks0[at])
        owned[s] = jnp.where(used > 0, block, jnp.zeros_like(block))
        copy = pltpu.make_async_copy(owned.at[s], owned_ref.at[s], owned_sem.at[s])
        copy.start()
        return copy

    half_done = PER_HALF + 2
    for step in range(ROUNDS + 2):
        if step < ROUNDS:
            products(step)
        if 0 <= step - 2 < ROUNDS:
            spread(step - 2)
        if 0 <= step - 1 < ROUNDS:
            between(step - 1)
        if 0 <= step - 3 < ROUNDS:
            pass_last(step - 3)
        if step == half_done:
            blocks_ready(0)
            precondition()
        if step < ROUNDS:
            merge1(step)
        if 0 <= step - 1 < ROUNDS:
            merge2(step - 1)
        if step == 0:
            roots_swap.wait_recv()
            routed.first()
            acts_first(1)
        if step == 1:
            acts_forward(1)
        if step == 2:
            routed.merge()
            acts_last(1)
        if step == half_done:
            for copy in swaps:
                copy.wait_recv()
            back.first()
        if step == half_done + 1:
            back.merge()
            routed.last(store_roots)
        if step == ROUNDS + 1:
            out_ref[1] = condition(holder_roots[0], blocks1[group], holder_roots[1])
        if 0 <= step - 2 < ROUNDS:
            pass_on(step - 2)
    back.last(store_update)
    pass_last(ROUNDS - 1)
    blocks_ready(1)
    kept = [collect(s) for s in range(CAP)]

    for copy in started:
        copy.wait_send()
    for r in range(ROUNDS - SLOTS, ROUNDS):
        for u in range(2):
            stages1[r, u].finish()
            stages2[r, u].finish()
    for copy in kept:
        copy.wait()


def gradient_blocks(owners, acts, grads_out, left_root, right_root):
    dma = pltpu.SemaphoreType.DMA
    piece, small, square, half = (2, PART, BLK), (PART // 2, BLK), (BLK, BLK), (HALF, BLK)
    shapes = [
        (BLK, SIDE * BLK),
        (2 * PER_HALF, SIDE * PART, BLK),
        (2, SIDE) + square,
        (SLOTS, 2, SIDE, 2) + piece,
        (SLOTS, 2, 2) + piece,
        (SLOTS, 2, 2, 2) + piece,
        (SLOTS, 2, SIDE, 2) + small,
        (SLOTS, 2, 2) + small,
        (SLOTS, 2, 2, 2) + small,
        (GROUPS,) + square,
        (GROUPS,) + square,
        (2, CAP) + square,
        (2, CAP) + square,
        (3, 2, 2) + half,
        (2, 2) + half,
        (2, 2, 2) + half,
        (2,) + square,
        (CAP,) + square,
        (CAP,) + square,
        (3, 2, 1) + half,
        (2, 1) + half,
        (2, 2, 1) + half,
        (CAP,) + square,
    ]
    semaphores = [
        (4,), (1,), (1,), (2, 4), (2, 4), (2, 3), (2, 3),
        (SLOTS, 2, 6), (SLOTS, 2, 6), (SLOTS, 2, 6), (SLOTS, 2, 6),
        (ROUNDS, 4), (ROUNDS, 4), (ROUNDS, 4), (ROUNDS, 4),
        (CAP,), (CAP,), (6,), (6,), (1,), (1,), (6,), (6,), (CAP,),
    ]
    return pl.pallas_call(
        gradient_kernel,
        out_shape=(
            jax.ShapeDtypeStruct((CAP, BLK, BLK), BF16),
            jax.ShapeDtypeStruct((2, BLK, BLK), BF16),
        ),
        in_specs=[pl.BlockSpec(memory_space=pltpu.SMEM)] + [pl.BlockSpec(memory_space=pl.ANY)] * 4,
        out_specs=(pl.BlockSpec(memory_space=pl.ANY), pl.BlockSpec(memory_space=pltpu.VMEM)),
        scratch_shapes=[pltpu.VMEM(shape, BF16) for shape in shapes]
        + [pltpu.SMEM((2 * GROUPS,), jnp.int32)] * 2
        + [dma(shape) for shape in semaphores],
        compiler_params=pltpu.CompilerParams(
            collective_id=0, has_side_effects=True, vmem_limit_bytes=62 << 20
        ),
        cost_estimate=pl.CostEstimate(flops=12 << 30, bytes_accessed=10 << 20, transcendentals=0),
        name="gradient_blocks",
    )(owners, acts, grads_out, left_root, right_root)


def grams_kernel(block_ref, ls_ref, rs_ref, ln_ref, rn_ref):
    block = block_ref[0]
    left = lax.dot_general(block, block, (((1,), (1,)), ((), ())), preferred_element_type=F32)
    ln_ref[0, 0, 0] = STAT_DECAY * ls_ref[0, 0, 0] + (1.0 - STAT_DECAY) * left
    right = lax.dot_general(block, block, (((0,), (0,)), ((), ())), preferred_element_type=F32)
    rn_ref[0, 0, 0] = STAT_DECAY * rs_ref[0, 0, 0] + (1.0 - STAT_DECAY) * right


def grams(owned, left_stats, right_stats):
    whole = pl.BlockSpec((1, 1, 1, BLK, BLK), lambda s: (0, 0, s, 0, 0))
    return pl.pallas_call(
        grams_kernel,
        grid=(CAP,),
        in_specs=[pl.BlockSpec((1, BLK, BLK), lambda s: (s, 0, 0)), whole, whole],
        out_specs=(whole, whole),
        out_shape=(
            jax.ShapeDtypeStruct(left_stats.shape, F32),
            jax.ShapeDtypeStruct(right_stats.shape, F32),
        ),
        compiler_params=pltpu.CompilerParams(vmem_limit_bytes=62 << 20),
        name="grams",
    )(owned, left_stats, right_stats)


def body(acts, grads_out, owners, left_stats, right_stats, left_root, right_root):
    owned, update = gradient_blocks(owners.reshape(-1), acts, grads_out, left_root, right_root)
    left_new, right_new = grams(owned, left_stats, right_stats)
    return (left_new, right_new, update)


def solution(mesh):
    placed = (
        P("dp", "group"),
        P("dp", "group"),
        P("dp", None, None),
        P("dp", "group", None, None, None),
        P("dp", "group", None, None, None),
        P("dp", "group", None, None, None),
        P("dp", "group", None, None, None),
    )
    return jax.shard_map(
        body,
        mesh=mesh,
        in_specs=placed,
        out_specs=(
            P("dp", "group", None, None, None),
            P("dp", "group", None, None, None),
            P(("group", "dp"), None, None),
        ),
        check_vma=False,
    )
```

```python
import functools

import jax
import jax.numpy as jnp
from jax import lax
from jax.experimental import pallas as pl
from jax.experimental.pallas import tpu as pltpu
from jax.sharding import PartitionSpec as P

MESH = pl.DeviceIdType.MESH
STAT_DECAY = 0.9
EPSILON = 1e-06
BLK = 512
HALF = BLK // 2
SIDE = 4
GROUPS = 8
CAP = 3
QUARTER = HALF // 2
TILE = BLK
SIZES = (64, 64, 64, 64, 64, 64, 64, 64)
ROUNDS = len(SIZES)
PER_HALF = ROUNDS // 2
LARGEST = max(SIZES)
STARTS = [2 * sum(SIZES[r - r % PER_HALF : r]) for r in range(ROUNDS)]
SLOTS = 4
MERGE1, BETWEEN, MERGE2, SPREAD, PASS_ON, PASS_LAST = 0, 1, 1, 2, 2, 3
F32 = jnp.float32
BF16 = jnp.bfloat16


def place():
    dp, group = lax.axis_index("dp"), lax.axis_index("group")
    return dp // SIDE, group // 2, lax.rem(dp, SIDE), lax.rem(group, 2)


def ring(index, step):
    return lax.rem(index + step + SIDE, SIDE)


def device(x, y, z, core):
    return (x * SIDE + z, y * 2 + core)


def remote(src, dst, send, recv, target):
    return pltpu.make_async_remote_copy(
        src_ref=src, dst_ref=dst, send_sem=send, recv_sem=recv, device_id=target, device_id_type=MESH
    )


def greet(targets):
    barrier = pltpu.get_barrier_semaphore()
    for target in targets:
        pl.semaphore_signal(barrier, inc=1, device_id=target, device_id_type=MESH)
    pl.semaphore_wait(barrier, len(targets))


def plus(*terms):
    total = terms[0].astype(F32)
    for term in terms[1:]:
        total = total + term.astype(F32)
    return total.astype(BF16)


class RingSum:
    def __init__(self, part, me, right, left, far, near, send, recv):
        self.part, self.me = part, me
        to_right = [
            (part(ring(me, 2)).at[0], far.at[0]),
            (part(ring(me, 1)).at[1], near.at[0, 1]),
            (part(ring(me, 1)).at[0], near.at[0, 0]),
        ]
        to_left = [
            (part(ring(me, 2)).at[1], far.at[1]),
            (part(ring(me, -1)).at[0], near.at[1, 0]),
            (part(ring(me, -1)).at[1], near.at[1, 1]),
        ]
        self.far, self.near = far, near
        self.copies = []
        for i in range(3):
            for j, (target, lists) in enumerate(((right, to_right), (left, to_left))):
                src, dst = lists[i]
                self.copies.append(remote(src, dst, send.at[2 * i + j], recv.at[2 * i + j], target))

    def first(self):
        for copy in self.copies[:4]:
            copy.start()

    def merge(self):
        for j, (step, half) in enumerate(((1, 0), (-1, 1))):
            self.copies[j].wait_recv()
            ref = self.part(ring(self.me, step)).at[half]
            ref[...] = plus(ref[...], self.far[j])
            self.copies[4 + j].start()

    def total(self):
        for copy in self.copies[2:]:
            copy.wait_recv()
        mine = self.part(self.me)
        return [plus(mine[half], self.near[0, half], self.near[1, half]) for half in range(2)]

    def finish(self):
        for copy in self.copies:
            copy.wait_send()


def gradient_kernel(
    owners, acts_ref, grads_ref, lr_ref, rr_ref,
    owned_ref, out_ref,
    grads, turned, acts, parts, far1, near1, sums, far2, near2, blocks0, blocks1,
    roots, pair_roots, roots_packed, roots_far, roots_near, holder_roots,
    result, held, packed, back_far, back_near, owned, slot_table, rank_table,
    local_sem, pair_send, pair_recv, acts_send, acts_recv, acts_cross_send, acts_cross_recv,
    send1, recv1, send2, recv2, out_send, out_recv, cross_send, cross_recv,
    swap_send, swap_recv, back_send, back_recv, roots_swap_send, roots_swap_recv, roots_send, roots_recv, owned_sem,
):
    x, y, z, core = place()
    group = y * 2 + core
    partner = device(x, y, z, 1 - core)
    along_y = [device(x, ring(y, s), z, core) for s in (1, -1)]
    along_x = [device(ring(x, s), y, z, core) for s in (1, -1)]
    along_z = [device(x, y, ring(z, s), core) for s in (1, -1)]
    blocks = (blocks0, blocks1)
    started = []

    def go(copy):
        copy.start()
        started.append(copy)
        return copy

    load_acts = pltpu.make_async_copy(acts_ref, acts.at[core, y], local_sem.at[0])
    load_grads = pltpu.make_async_copy(grads_ref, grads, local_sem.at[1])
    load_roots = [
        pltpu.make_async_copy(ref.at[0, 0], roots.at[i], local_sem.at[2 + i]) for i, ref in enumerate((lr_ref, rr_ref))
    ]
    load_acts.start()
    load_grads.start()
    for copy in load_roots:
        copy.start()
    greet([partner] + along_y + along_x + along_z)

    load_acts.wait()
    own = acts.at[core, y]
    pair = go(remote(own, own, pair_send.at[0], pair_recv.at[0], partner))
    gathers = {}

    def rows_of(h, at, start, size):
        return acts.at[h, at, pl.ds(pl.multiple_of(core * HALF + start, 16), size)]

    def acts_first(h):
        gathers[h] = []
        for i in range(2):
            for j in range(2):
                here = rows_of(h, y, (i ^ j) * QUARTER, QUARTER)
                n = 2 * i + j
                gathers[h].append(go(remote(here, here, acts_send.at[h, n], acts_recv.at[h, n], along_y[j])))
        gathers[h, "cross"] = []

    def acts_cross(h, i, at):
        here = rows_of(h, at, 0, HALF)
        gathers[h, "cross"].append(
            go(remote(here, here, acts_cross_send.at[h, i], acts_cross_recv.at[h, i], partner))
        )

    def acts_forward(h):
        for j in range(2):
            gathers[h][j].wait_recv()
            here = rows_of(h, ring(y, (-1, 1)[j]), j * QUARTER, QUARTER)
            n = 4 + j
            gathers[h].append(go(remote(here, here, acts_send.at[h, n], acts_recv.at[h, n], along_y[j])))
        for j in range(2):
            gathers[h][2 + j].wait_recv()
            acts_cross(h, j, ring(y, (-1, 1)[j]))

    def acts_last(h):
        for copy in gathers[h][4:]:
            copy.wait_recv()
        acts_cross(h, 2, ring(y, 2))

    def acts_ready(h):
        for copy in gathers[h, "cross"]:
            copy.wait_recv()

    pair.wait_recv()
    acts_first(0)

    count = 2 * GROUPS
    owner = [owners[k] for k in range(count)]
    zero, one = jnp.int32(0), jnp.int32(1)
    slot, rank = [], []
    for k in range(count):
        same = [jnp.where(owner[k2] == owner[k], one, zero) for k2 in range(k)]
        slot.append(sum(same, zero))
        rank.append(sum(same[0::2], zero))
        slot_table[k] = jnp.minimum(slot[k], CAP - 1)
        rank_table[k] = jnp.minimum(rank[k], CAP - 1)
    is_mine = [owner[k] == group for k in range(count)]

    def pick(positions, test, value):
        return sum([jnp.where(is_mine[k] & test(k), value(k), zero) for k in positions], zero)

    load_grads.wait()
    for xd in range(SIDE):
        for start in range(0, BLK, QUARTER):
            turned[xd, start : start + QUARTER, :] = grads[:, xd * BLK + start : xd * BLK + start + QUARTER].T
    acts_forward(0)
    for copy in load_roots:
        copy.wait()
    acts_last(0)
    roots_swap = go(remote(roots, pair_roots, roots_swap_send.at[0], roots_swap_recv.at[0], partner))

    stages1, stages2, outs, crosses = {}, {}, {}, {}

    def products(r):
        p, b, size = r // PER_HALF, r % SLOTS, SIZES[r]
        if r % PER_HALF == 0:
            acts_ready(p)
        for u in range(2):
            if r >= SLOTS:
                stages1[r - SLOTS, u].finish()
            left = turned[:, STARTS[r] + u * size : STARTS[r] + (u + 1) * size, :].reshape(SIDE * size, BLK)

            def step(zd, carry, u=u, left=left):
                value = jnp.dot(left, acts[p, zd], preferred_element_type=F32).astype(BF16)
                for xd in range(SIDE):
                    piece = value[xd * size : (xd + 1) * size]
                    if u == 0:
                        parts[b, 0, xd, zd // 2, lax.rem(zd, 2), 0:size] = piece
                    else:
                        parts[b, 1, zd, xd // 2, xd % 2, 0:size] = piece
                return carry

            lax.fori_loop(0, SIDE, step, 0)
            me, (right, left_to) = ((x, along_x), (z, along_z))[u]
            rows = pl.ds(0, size)
            stage = RingSum(
                lambda d, u=u: parts.at[b, u, d, :, :, rows], me, right, left_to,
                far1.at[b, u, :, :, rows], near1.at[b, u, :, :, :, rows], send1.at[b, u], recv1.at[b, u],
            )
            stage.first()
            stages1[r, u] = stage

    def merge1(r):
        for u in range(2):
            stages1[r, u].merge()

    def between(r):
        b, size = r % SLOTS, SIZES[r] // 2
        for u in range(2):
            if r >= SLOTS:
                stages2[r - SLOTS, u].finish()
            total = stages1[r, u].total()
            for half in range(2):
                for o in range(2):
                    for piece in range(2):
                        sums[b, u, half * 2 + o, piece, 0:size] = total[half][o, piece * size : (piece + 1) * size]
            me, (right, left_to) = ((z, along_z), (x, along_x))[u]
            rows = pl.ds(0, size)
            stage = RingSum(
                lambda d, u=u: sums.at[b, u, d, :, rows], me, right, left_to,
                far2.at[b, u, :, rows], near2.at[b, u, :, :, rows], send2.at[b, u], recv2.at[b, u],
            )
            stage.first()
            stages2[r, u] = stage

    def merge2(r):
        for u in range(2):
            stages2[r, u].merge()

    def strip(r, at, start, size):
        return blocks[r // PER_HALF].at[at, pl.ds(STARTS[r] + start, size)]

    def cross(r, i, at):
        here = strip(r, at, 0, 2 * SIZES[r])
        crosses[r].append(go(remote(here, here, cross_send.at[r, i], cross_recv.at[r, i], partner)))

    def spread(r):
        p, size = r // PER_HALF, SIZES[r]
        for u in range(2):
            total = stages2[r, u].total()
            for half in range(2):
                start = STARTS[r] + u * size + half * (size // 2)
                blocks[p][group, start : start + size // 2] = total[half]
        outs[r], crosses[r] = [], []
        for i in range(2):
            for j in range(2):
                here, n = strip(r, group, (i ^ j) * size, size), 2 * i + j
                outs[r].append(go(remote(here, here, out_send.at[r, n], out_recv.at[r, n], along_y[j])))
        cross(r, 0, group)

    def pass_on(r):
        for j in range(2):
            outs[r][j].wait_recv()
            here, n = strip(r, 2 * ring(y, (-1, 1)[j]) + core, j * SIZES[r], SIZES[r]), 4 + j
            outs[r].append(go(remote(here, here, out_send.at[r, n], out_recv.at[r, n], along_y[j])))
        for j in range(2):
            outs[r][2 + j].wait_recv()
            cross(r, 1 + j, 2 * ring(y, (-1, 1)[j]) + core)

    def pass_last(r):
        for copy in outs[r][4:]:
            copy.wait_recv()
        cross(r, 3, 2 * ring(y, 2) + core)

    def blocks_ready(p):
        for r in range(p * PER_HALF, (p + 1) * PER_HALF):
            for copy in crosses[r]:
                copy.wait_recv()

    def condition(left_root, block, right_root):
        shaped = jnp.dot(left_root, block, preferred_element_type=F32).astype(BF16)
        product = jnp.dot(shaped, right_root, preferred_element_type=F32)
        scaling = lax.rsqrt(jnp.mean(product * product) + EPSILON)
        return (product * scaling).astype(BF16)

    swaps = []

    def precondition():
        for j in range(CAP):
            def test(k, j=j):
                return rank[k] == j

            even = range(0, count, 2)
            which, at = pick(even, test, lambda k: jnp.int32(k // 2)), pick(even, test, lambda k: jnp.minimum(slot[k], CAP - 1))
            result[j] = condition(roots[0, at], blocks0[which], roots[1, at])
            swaps.append(go(remote(result.at[j], held.at[j], swap_send.at[j], swap_recv.at[j], partner)))

    class Routed:
        def __init__(self, parity, table, sources, packed, far, near, send, recv):
            self.parity, self.table, self.sources = parity, table, sources
            self.packed, self.far, self.near = packed, far, near
            self.order = (((2, 0), (2, 1)), ((1, 1), (-1, 0)), ((1, 0), (-1, 1)))
            landing = ((far.at[0], far.at[1]), (near.at[0, 1], near.at[1, 0]), (near.at[0, 0], near.at[1, 1]))
            self.copies = [
                remote(packed.at[i, j], landing[i][j], send.at[2 * i + j], recv.at[2 * i + j], along_y[j])
                for i in range(3)
                for j in range(2)
            ]

        def mine(self, step, half):
            k = 2 * (2 * ring(y, step) + core) + self.parity
            owner, at = owners[k], self.table[k]
            rows = pl.ds(half * HALF, HALF)
            return [
                jnp.where(lax.rem(owner, 2) == core, here(at, rows), there(at, rows)) for here, there in self.sources
            ], owner // 2

        def send(self, i):
            for j in range(2):
                for n, value in enumerate(self.mine(*self.order[i][j])[0]):
                    self.packed[i, j, n] = value
                go(self.copies[2 * i + j])

        def merge(self):
            for j in range(2):
                self.copies[j].wait_recv()
                values, at = self.mine(*self.order[2][j])
                for n, value in enumerate(values):
                    self.packed[2, j, n] = jnp.where(at == y, value, self.far[j, n])
                go(self.copies[4 + j])

        def last(self, store):
            for copy in self.copies[2:]:
                copy.wait_recv()
            for half in range(2):
                values, at = self.mine(0, half)
                from_left = at == ring(y, -1)
                if half == 0:
                    from_left = from_left | (at == ring(y, 2))
                for n, value in enumerate(values):
                    arrived = jnp.where(from_left, self.near[0, half, n], self.near[1, half, n])
                    store(n, half, jnp.where(at == y, value, arrived))

    back = Routed(
        0, rank_table, [(lambda at, rows: result[at, rows], lambda at, rows: held[at, rows])],
        packed, back_far, back_near, back_send, back_recv,
    )
    routed = [
        Routed(
            1, slot_table,
            [(lambda at, rows, n=n: roots[n, at, rows], lambda at, rows, n=n: pair_roots[n, at, rows])],
            roots_packed.at[n], roots_far.at[n], roots_near.at[n], roots_send.at[n], roots_recv.at[n],
        )
        for n in range(2)
    ]

    def store_roots(side, _, half, value):
        holder_roots[side, half * HALF : (half + 1) * HALF] = value

    def store_update(n, half, value):
        out_ref[0, half * HALF : (half + 1) * HALF] = value

    def collect(s):
        def test(k):
            return slot[k] == s

        every = range(count)
        odd = pick(every, test, lambda k: jnp.int32(k % 2))
        at = pick(every, test, lambda k: jnp.int32(k // 2))
        used = pick(every, test, lambda k: one)
        block = jnp.where(odd > 0, blocks1[at], blocks0[at])
        owned[s] = jnp.where(used > 0, block, jnp.zeros_like(block))
        copy = pltpu.make_async_copy(owned.at[s], owned_ref.at[s], owned_sem.at[s])
        copy.start()
        return copy

    half_done = PER_HALF - 1 + PASS_LAST

    def at_lag(part, lag):
        if 0 <= step - lag < ROUNDS:
            part(step - lag)

    for step in range(ROUNDS + PASS_LAST):
        at_lag(products, 0)
        at_lag(spread, SPREAD)
        at_lag(pass_last, PASS_LAST)
        at_lag(between, BETWEEN)
        if step == half_done:
            blocks_ready(0)
            precondition()
        at_lag(merge1, MERGE1)
        at_lag(merge2, MERGE2)
        if step == ROUNDS - 1 + SPREAD:
            out_ref[1] = condition(holder_roots[0], blocks1[group], holder_roots[1])
        at_lag(pass_on, PASS_ON)
        if step == 0:
            acts_first(1)
            roots_swap.wait_recv()
            routed[0].send(0)
        if step == 1:
            acts_forward(1)
            routed[0].send(1)
        if step == 2:
            acts_last(1)
            routed[0].merge()
        if step == 3:
            routed[1].send(0)
        if step == 4:
            routed[1].send(1)
        if step == 5:
            routed[1].merge()
        if step == half_done:
            for copy in swaps:
                copy.wait_recv()
            back.send(0)
            back.send(1)
        if step == ROUNDS - 1:
            for n in range(2):
                routed[n].last(functools.partial(store_roots, n))
        if step == half_done + 1:
            back.merge()
    back.last(store_update)
    blocks_ready(1)
    kept = [collect(s) for s in range(CAP)]

    for copy in started:
        copy.wait_send()
    for r in range(ROUNDS - SLOTS, ROUNDS):
        for u in range(2):
            stages1[r, u].finish()
            stages2[r, u].finish()
    for copy in kept:
        copy.wait()


def gradient_blocks(owners, acts, grads_out, left_root, right_root):
    dma = pltpu.SemaphoreType.DMA
    piece, small, square, half = (2, LARGEST, BLK), (LARGEST // 2, BLK), (BLK, BLK), (HALF, BLK)
    shapes = [
        (BLK, SIDE * BLK),
        (SIDE,) + square,
        (2, SIDE) + square,
        (SLOTS, 2, SIDE, 2) + piece,
        (SLOTS, 2, 2) + piece,
        (SLOTS, 2, 2, 2) + piece,
        (SLOTS, 2, SIDE, 2) + small,
        (SLOTS, 2, 2) + small,
        (SLOTS, 2, 2, 2) + small,
        (GROUPS,) + square,
        (GROUPS,) + square,
        (2, CAP) + square,
        (2, CAP) + square,
        (2, 3, 2, 1) + half,
        (2, 2, 1) + half,
        (2, 2, 2, 1) + half,
        (2,) + square,
        (CAP,) + square,
        (CAP,) + square,
        (3, 2, 1) + half,
        (2, 1) + half,
        (2, 2, 1) + half,
        (CAP,) + square,
    ]
    semaphores = [
        (4,), (1,), (1,), (2, 6), (2, 6), (2, 3), (2, 3),
        (SLOTS, 2, 6), (SLOTS, 2, 6), (SLOTS, 2, 6), (SLOTS, 2, 6),
        (ROUNDS, 6), (ROUNDS, 6), (ROUNDS, 4), (ROUNDS, 4),
        (CAP,), (CAP,), (6,), (6,), (1,), (1,), (2, 6), (2, 6), (CAP,),
    ]
    return pl.pallas_call(
        gradient_kernel,
        out_shape=(
            jax.ShapeDtypeStruct((CAP, BLK, BLK), BF16),
            jax.ShapeDtypeStruct((2, BLK, BLK), BF16),
        ),
        in_specs=[pl.BlockSpec(memory_space=pltpu.SMEM)] + [pl.BlockSpec(memory_space=pl.ANY)] * 4,
        out_specs=(pl.BlockSpec(memory_space=pl.ANY), pl.BlockSpec(memory_space=pltpu.VMEM)),
        scratch_shapes=[pltpu.VMEM(shape, BF16) for shape in shapes]
        + [pltpu.SMEM((2 * GROUPS,), jnp.int32)] * 2
        + [dma(shape) for shape in semaphores],
        compiler_params=pltpu.CompilerParams(
            collective_id=0, has_side_effects=True, vmem_limit_bytes=62 << 20
        ),
        cost_estimate=pl.CostEstimate(flops=12 << 30, bytes_accessed=10 << 20, transcendentals=0),
        name="gradient_blocks",
    )(owners, acts, grads_out, left_root, right_root)


def grams_kernel(block_ref, ls_ref, rs_ref, ln_ref, rn_ref):
    block = block_ref[0]
    rows = pl.ds(pl.multiple_of(pl.program_id(1) * TILE, TILE), TILE)
    left = lax.dot_general(block_ref[0, rows], block, (((1,), (1,)), ((), ())), preferred_element_type=F32)
    ln_ref[0, 0, 0] = STAT_DECAY * ls_ref[0, 0, 0] + (1.0 - STAT_DECAY) * left
    right = lax.dot_general(block_ref[0, :, rows], block, (((0,), (0,)), ((), ())), preferred_element_type=F32)
    rn_ref[0, 0, 0] = STAT_DECAY * rs_ref[0, 0, 0] + (1.0 - STAT_DECAY) * right


def grams(owned, left_stats, right_stats):
    part = pl.BlockSpec((1, 1, 1, TILE, BLK), lambda s, i: (0, 0, s, i, 0))
    return pl.pallas_call(
        grams_kernel,
        grid=(CAP, BLK // TILE),
        in_specs=[pl.BlockSpec((1, BLK, BLK), lambda s, i: (s, 0, 0)), part, part],
        out_specs=(part, part),
        out_shape=(
            jax.ShapeDtypeStruct(left_stats.shape, F32),
            jax.ShapeDtypeStruct(right_stats.shape, F32),
        ),
        compiler_params=pltpu.CompilerParams(vmem_limit_bytes=62 << 20),
        name="grams",
    )(owned, left_stats, right_stats)


def body(acts, grads_out, owners, left_stats, right_stats, left_root, right_root):
    owned, update = gradient_blocks(owners.reshape(-1), acts, grads_out, left_root, right_root)
    left_new, right_new = grams(owned, left_stats, right_stats)
    return (left_new, right_new, update)


def solution(mesh):
    placed = (
        P("dp", "group"),
        P("dp", "group"),
        P("dp", None, None),
        P("dp", "group", None, None, None),
        P("dp", "group", None, None, None),
        P("dp", "group", None, None, None),
        P("dp", "group", None, None, None),
    )
    return jax.shard_map(
        body,
        mesh=mesh,
        in_specs=placed,
        out_specs=(
            P("dp", "group", None, None, None),
            P("dp", "group", None, None, None),
            P(("group", "dp"), None, None),
        ),
        check_vma=False,
    )
```

```python
import functools

import jax
import jax.numpy as jnp
from jax import lax
from jax.experimental import pallas as pl
from jax.experimental.pallas import tpu as pltpu
from jax.sharding import PartitionSpec as P

MESH = pl.DeviceIdType.MESH
STAT_DECAY = 0.9
EPSILON = 1e-06
BLK = 512
HALF = BLK // 2
SIDE = 4
GROUPS = 8
CAP = 3
QUARTER = HALF // 2
TILE = BLK
COLS = 128
PER_HALF = BLK // COLS
ROUNDS = 2 * PER_HALF
SLOTS = 3
F32 = jnp.float32
BF16 = jnp.bfloat16


def place():
    dp, group = lax.axis_index("dp"), lax.axis_index("group")
    return dp // SIDE, group // 2, lax.rem(dp, SIDE), lax.rem(group, 2)


def ring(index, step):
    return lax.rem(index + step + SIDE, SIDE)


def device(x, y, z, core):
    return (x * SIDE + z, y * 2 + core)


def remote(src, dst, send, recv, target):
    return pltpu.make_async_remote_copy(
        src_ref=src, dst_ref=dst, send_sem=send, recv_sem=recv, device_id=target, device_id_type=MESH
    )


def greet(targets):
    barrier = pltpu.get_barrier_semaphore()
    for target in targets:
        pl.semaphore_signal(barrier, inc=1, device_id=target, device_id_type=MESH)
    pl.semaphore_wait(barrier, len(targets))


def plus(*terms):
    total = terms[0].astype(F32)
    for term in terms[1:]:
        total = total + term.astype(F32)
    return total.astype(BF16)


class RingSum:
    def __init__(self, parts, me, right, left, far, near, send, recv):
        self.parts, self.me, self.far, self.near = parts, me, far, near

        def copy(d, half, dst, recv_sem, target):
            return remote(parts.at[ring(me, d), half], dst, send, recv_sem, target)

        self.copies = [
            copy(2, 0, far.at[0], recv.at[0], right),
            copy(2, 1, far.at[1], recv.at[1], left),
            copy(1, 1, near.at[0, 1], recv.at[2], right),
            copy(-1, 0, near.at[1, 0], recv.at[2], left),
            copy(1, 0, near.at[0, 0], recv.at[2], right),
            copy(-1, 1, near.at[1, 1], recv.at[2], left),
        ]
        sent = parts.at[pl.ds(0, SIDE - 1)]
        self.all_sent = remote(sent, sent, send, recv.at[2], right)
        self.all_near = remote(near, near, send, recv.at[2], right)

    def first(self):
        for copy in self.copies[:4]:
            copy.start()

    def merge(self):
        for j, (step, half) in enumerate(((1, 0), (-1, 1))):
            self.copies[j].wait_recv()
            at = ring(self.me, step)
            self.parts[at, half] = plus(self.parts[at, half], self.far[j])
            self.copies[4 + j].start()

    def total(self):
        self.all_near.wait_recv()
        return [plus(self.parts[self.me, half], self.near[0, half], self.near[1, half]) for half in range(2)]

    def finish(self):
        self.all_sent.wait_send()


class Routed:
    def __init__(self, parity, owners, table, y, core, along_y, here, there, packed, far, near, send, recv):
        self.parity, self.owners, self.table, self.y, self.core = parity, owners, table, y, core
        self.here, self.there, self.packed, self.far, self.near = here, there, packed, far, near
        self.order = (((2, 0), (2, 1)), ((1, 1), (-1, 0)), ((1, 0), (-1, 1)))
        landing = ((far.at[0], far.at[1]), (near.at[0, 1], near.at[1, 0]), (near.at[0, 0], near.at[1, 1]))
        self.copies = [
            remote(packed.at[i, j], landing[i][j], send, recv.at[j if i == 0 else 2], along_y[j])
            for i in range(3)
            for j in range(2)
        ]
        self.all_sent = remote(packed, packed, send, recv.at[2], along_y[0])
        self.all_near = remote(near, near, send, recv.at[2], along_y[0])

    def mine(self, step, half):
        k = 2 * (2 * ring(self.y, step) + self.core) + self.parity
        owner, at = self.owners[k], self.table[k]
        rows = pl.ds(half * HALF, HALF)
        return jnp.where(lax.rem(owner, 2) == self.core, self.here[at, rows], self.there[at, rows]), owner // 2

    def send(self, i):
        for j in range(2):
            self.packed[i, j] = self.mine(*self.order[i][j])[0]
            self.copies[2 * i + j].start()

    def merge(self):
        for j in range(2):
            self.copies[j].wait_recv()
            value, at = self.mine(*self.order[2][j])
            self.packed[2, j] = jnp.where(at == self.y, value, self.far[j])
            self.copies[4 + j].start()

    def last(self, out):
        self.all_near.wait_recv()
        for half in range(2):
            value, at = self.mine(0, half)
            from_left = at == ring(self.y, -1)
            if half == 0:
                from_left = from_left | (at == ring(self.y, 2))
            arrived = jnp.where(from_left, self.near[0, half], self.near[1, half])
            out[half * HALF : (half + 1) * HALF] = jnp.where(at == self.y, value, arrived)

    def finish(self):
        self.all_sent.wait_send()


def gradient_kernel(
    owners, acts_ref, grads_ref, lr_ref, rr_ref,
    owned_ref, out_ref,
    grads, turned, acts, parts, far1, near1, sums, far2, near2, blocks0, blocks1,
    roots, pair_roots, roots_packed, roots_far, roots_near, holder_roots, owned, slot_table,
    local_sem, pair_send, pair_recv, acts_send, acts_recv, acts_cross_send, acts_cross_recv,
    send1, recv1, send2, recv2, out_send, out_recv, cross_send, cross_recv,
    roots_swap_send, roots_swap_recv, roots_send, roots_recv, owned_sem,
):
    x, y, z, core = place()
    group = y * 2 + core
    partner = device(x, y, z, 1 - core)
    along_y = [device(x, ring(y, s), z, core) for s in (1, -1)]
    along_x = [device(ring(x, s), y, z, core) for s in (1, -1)]
    along_z = [device(x, y, ring(z, s), core) for s in (1, -1)]
    blocks = (blocks0, blocks1)
    started = []

    def go(copy):
        copy.start()
        started.append(copy)
        return copy

    load_acts = [
        pltpu.make_async_copy(acts_ref.at[:, pl.ds(v * COLS, COLS)], acts.at[core, v, y], local_sem.at[v])
        for v in range(PER_HALF)
    ]
    load_grads = pltpu.make_async_copy(grads_ref, grads, local_sem.at[PER_HALF])
    load_roots = [
        pltpu.make_async_copy(ref.at[0, 0], roots.at[i], local_sem.at[PER_HALF + 1 + i])
        for i, ref in enumerate((lr_ref, rr_ref))
    ]
    for copy in load_acts + [load_grads] + load_roots:
        copy.start()
    greet([partner] + along_y + along_x + along_z)

    for copy in load_acts:
        copy.wait()
    own = acts.at[core, :, y]
    pair = go(remote(own, own, pair_send.at[0], pair_recv.at[0], partner))
    spans = ((0, 0, 1), (0, 1, PER_HALF - 1), (1, 0, PER_HALF))
    gathers, gather_crosses = {}, {}

    def tokens(g, at, start, size):
        h, first, number = spans[g]
        return acts.at[h, pl.ds(first, number), at, pl.ds(pl.multiple_of(core * HALF + start, 16), size)]

    def acts_first(g):
        gathers[g], gather_crosses[g] = [], []
        for i in range(2):
            for j in range(2):
                here, n = tokens(g, y, (i ^ j) * QUARTER, QUARTER), 2 * i + j
                gathers[g].append(go(remote(here, here, acts_send.at[g, n], acts_recv.at[g, n], along_y[j])))

    def acts_cross(g, i, at):
        here = tokens(g, at, 0, HALF)
        gather_crosses[g].append(
            go(remote(here, here, acts_cross_send.at[g, i], acts_cross_recv.at[g, i], partner))
        )

    def acts_forward(g):
        for j in range(2):
            gathers[g][j].wait_recv()
            here, n = tokens(g, ring(y, (-1, 1)[j]), j * QUARTER, QUARTER), 4 + j
            gathers[g].append(go(remote(here, here, acts_send.at[g, n], acts_recv.at[g, n], along_y[j])))
        for j in range(2):
            gathers[g][2 + j].wait_recv()
            acts_cross(g, j, ring(y, (-1, 1)[j]))

    def acts_last(g):
        for copy in gathers[g][4:]:
            copy.wait_recv()
        acts_cross(g, 2, ring(y, 2))

    def acts_ready(g):
        for copy in gather_crosses[g]:
            copy.wait_recv()

    pair.wait_recv()
    acts_first(0)
    acts_first(1)

    count = 2 * GROUPS
    owner = [owners[k] for k in range(count)]
    zero, one = jnp.int32(0), jnp.int32(1)
    slot = []
    for k in range(count):
        slot.append(sum([jnp.where(owner[k2] == owner[k], one, zero) for k2 in range(k)], zero))
        slot_table[k] = jnp.minimum(slot[k], CAP - 1)

    load_grads.wait()
    for xd in range(SIDE):
        for start in range(0, BLK, QUARTER):
            turned[xd, start : start + QUARTER, :] = grads[:, xd * BLK + start : xd * BLK + start + QUARTER].T
    acts_forward(0)
    for copy in load_roots:
        copy.wait()
    acts_last(0)
    roots_swap = go(remote(roots, pair_roots, roots_swap_send.at[0], roots_swap_recv.at[0], partner))

    stages1, stages2, outs, crosses = {}, {}, {}, {}

    def products(r):
        p, v, b = r // PER_HALF, r % PER_HALF, r % SLOTS
        if r < 2:
            acts_ready(r)
        if r == PER_HALF:
            acts_ready(2)
        right = jnp.concatenate([acts[p, v, zd] for zd in range(SIDE)], axis=1)
        for u in range(2):
            if r >= SLOTS:
                stages1[r - SLOTS, u].finish()

            def step(xd, carry, u=u):
                left = turned[xd, u * HALF : (u + 1) * HALF]
                value = jnp.dot(left, right, preferred_element_type=F32).astype(BF16)
                for half in range(2):
                    rows = value[half * QUARTER : (half + 1) * QUARTER]
                    if u == 0:
                        parts[b, 0, xd, half] = rows
                    else:
                        lanes = pl.ds(pl.multiple_of(xd * COLS, COLS), COLS)
                        for zd in range(SIDE):
                            parts[b, 1, zd, half, :, lanes] = rows[:, zd * COLS : (zd + 1) * COLS]
                return carry

            lax.fori_loop(0, SIDE, step, 0)
            me, (right_to, left_to) = ((x, along_x), (z, along_z))[u]
            stage = RingSum(
                parts.at[b, u], me, right_to, left_to, far1.at[b, u], near1.at[b, u], send1.at[b, u], recv1.at[b, u]
            )
            stage.first()
            stages1[r, u] = stage

    def merge1(r):
        for u in range(2):
            stages1[r, u].merge()

    def between(r):
        b = r % SLOTS
        for u in range(2):
            if r >= SLOTS:
                stages2[r - SLOTS, u].finish()
            total = stages1[r, u].total()
            for half in range(2):
                for d in range(SIDE):
                    sums[b, u, d, half] = total[half][:, d * COLS : (d + 1) * COLS]
            me, (right_to, left_to) = ((z, along_z), (x, along_x))[u]
            stage = RingSum(
                sums.at[b, u], me, right_to, left_to, far2.at[b, u], near2.at[b, u], send2.at[b, u], recv2.at[b, u]
            )
            stage.first()
            stages2[r, u] = stage

    def merge2(r):
        for u in range(2):
            stages2[r, u].merge()

    def strip(r, at, half):
        return blocks[r // PER_HALF].at[core, at, r % PER_HALF, pl.ds(half * HALF, HALF)]

    def spread(r):
        for u in range(2):
            total = stages2[r, u].total()
            for half in range(2):
                start = u * HALF + half * QUARTER
                blocks[r // PER_HALF][core, y, r % PER_HALF, start : start + QUARTER] = total[half]
        outs[r] = []
        for i in range(2):
            for j in range(2):
                here = strip(r, y, i ^ j)
                outs[r].append(remote(here, here, out_send.at[r], out_recv.at[r, 2 * i + j], along_y[j]))
                outs[r][-1].start()

    def pass_on(r):
        for j in range(2):
            outs[r][j].wait_recv()
            here = strip(r, ring(y, (-1, 1)[j]), j)
            outs[r].append(remote(here, here, out_send.at[r], out_recv.at[r, 4 + j], along_y[j]))
            outs[r][-1].start()

    def pass_last(r):
        for copy in outs[r][2:]:
            copy.wait_recv()
        here = blocks[r // PER_HALF].at[core, :, r % PER_HALF]
        crosses[r] = go(remote(here, here, cross_send.at[r], cross_recv.at[r], partner))

    def spread_finish(r):
        sent = blocks[r // PER_HALF].at[core, pl.ds(0, SIDE - 1), r % PER_HALF]
        remote(sent, sent, out_send.at[r], out_recv.at[r, 0], partner).wait_send()

    def whole(p, c, at):
        return jnp.concatenate([blocks[p][c, at, v] for v in range(PER_HALF)], axis=1)

    def hold(p):
        shaped = jnp.dot(holder_roots[p, 0], whole(p, core, y), preferred_element_type=F32).astype(BF16)
        product = jnp.dot(shaped, holder_roots[p, 1], preferred_element_type=F32)
        scaling = lax.rsqrt(jnp.mean(product * product) + EPSILON)
        out_ref[p] = (product * scaling).astype(BF16)

    routed = [
        [
            Routed(
                p, owners, slot_table, y, core, along_y, roots.at[n], pair_roots.at[n],
                roots_packed.at[n], roots_far.at[p, n], roots_near.at[p, n], roots_send.at[p, n], roots_recv.at[p, n],
            )
            for n in range(2)
        ]
        for p in range(2)
    ]
    (left0, right0), (left1, right1) = routed

    def collect(s):
        def pick(value):
            return sum([jnp.where((owner[k] == group) & (slot[k] == s), value(k), zero) for k in range(count)], zero)

        odd, used = pick(lambda k: jnp.int32(k % 2)), pick(lambda k: one)
        c, at = pick(lambda k: jnp.int32(k // 2 % 2)), pick(lambda k: jnp.int32(k // 4))
        block = jnp.where(odd > 0, whole(1, c, at), whole(0, c, at))
        owned[s] = jnp.where(used > 0, block, jnp.zeros_like(block))
        copy = pltpu.make_async_copy(owned.at[s], owned_ref.at[s], owned_sem.at[s])
        copy.start()
        return copy

    def at_lag(part, lag):
        if 0 <= step - lag < ROUNDS:
            part(step - lag)

    for step in range(ROUNDS + 4):
        at_lag(products, 0)
        at_lag(spread, 2)
        at_lag(pass_last, 4)
        at_lag(between, 1)
        at_lag(merge1, 0)
        at_lag(merge2, 1)
        at_lag(pass_on, 3)
        if step == 0:
            acts_forward(1)
            roots_swap.wait_recv()
            left1.send(0)
            acts_last(1)
        if step == 1:
            acts_first(2)
            left1.send(1)
        if step == 2:
            acts_forward(2)
            left1.merge()
        if step == 3:
            acts_last(2)
            right1.send(0)
        if step == 4:
            right1.send(1)
            left1.finish()
            left0.send(0)
        if step == 5:
            right1.merge()
        if step == 6:
            left0.send(1)
            right1.finish()
            right0.send(0)
        if step == 7:
            left0.merge()
            right0.send(1)
            left1.last(holder_roots.at[1, 0])
            right1.last(holder_roots.at[1, 1])
        if step == 8:
            right0.merge()
        if step == 9:
            hold(1)
        if step == 10:
            left0.last(holder_roots.at[0, 0])
            right0.last(holder_roots.at[0, 1])
            hold(0)
    for r in range(ROUNDS):
        crosses[r].wait_recv()
    kept = [collect(s) for s in range(CAP)]

    for copy in started:
        copy.wait_send()
    left0.finish()
    right0.finish()
    for r in range(ROUNDS):
        spread_finish(r)
    for r in range(ROUNDS - SLOTS, ROUNDS):
        for u in range(2):
            stages1[r, u].finish()
            stages2[r, u].finish()
    for copy in kept:
        copy.wait()


def gradient_blocks(owners, acts, grads_out, left_root, right_root):
    dma = pltpu.SemaphoreType.DMA
    square, half, wide, small = (BLK, BLK), (HALF, BLK), (QUARTER, BLK), (QUARTER, COLS)
    shapes = [
        (BLK, SIDE * BLK),
        (SIDE,) + square,
        (2, PER_HALF, SIDE, BLK, COLS),
        (SLOTS, 2, SIDE, 2) + wide,
        (SLOTS, 2, 2) + wide,
        (SLOTS, 2, 2, 2) + wide,
        (SLOTS, 2, SIDE, 2) + small,
        (SLOTS, 2, 2) + small,
        (SLOTS, 2, 2, 2) + small,
        (2, SIDE, PER_HALF, BLK, COLS),
        (2, SIDE, PER_HALF, BLK, COLS),
        (2, CAP) + square,
        (2, CAP) + square,
        (2, 3, 2) + half,
        (2, 2, 2) + half,
        (2, 2, 2, 2) + half,
        (2, 2) + square,
        (CAP,) + square,
    ]
    semaphores = [
        (PER_HALF + 3,), (1,), (1,), (3, 6), (3, 6), (3, 3), (3, 3),
        (SLOTS, 2), (SLOTS, 2, 3), (SLOTS, 2), (SLOTS, 2, 3),
        (ROUNDS,), (ROUNDS, 6), (ROUNDS,), (ROUNDS,),
        (1,), (1,), (2, 2), (2, 2, 3), (CAP,),
    ]
    return pl.pallas_call(
        gradient_kernel,
        out_shape=(
            jax.ShapeDtypeStruct((CAP, BLK, BLK), BF16),
            jax.ShapeDtypeStruct((2, BLK, BLK), BF16),
        ),
        in_specs=[pl.BlockSpec(memory_space=pltpu.SMEM)] + [pl.BlockSpec(memory_space=pl.ANY)] * 4,
        out_specs=(pl.BlockSpec(memory_space=pl.ANY), pl.BlockSpec(memory_space=pltpu.VMEM)),
        scratch_shapes=[pltpu.VMEM(shape, BF16) for shape in shapes]
        + [pltpu.SMEM((2 * GROUPS,), jnp.int32)]
        + [dma(shape) for shape in semaphores],
        compiler_params=pltpu.CompilerParams(
            collective_id=0, has_side_effects=True, vmem_limit_bytes=62 << 20
        ),
        cost_estimate=pl.CostEstimate(flops=12 << 30, bytes_accessed=10 << 20, transcendentals=0),
        name="gradient_blocks",
    )(owners, acts, grads_out, left_root, right_root)


def grams_kernel(block_ref, ls_ref, rs_ref, ln_ref, rn_ref):
    block = block_ref[0]
    rows = pl.ds(pl.multiple_of(pl.program_id(1) * TILE, TILE), TILE)
    left = lax.dot_general(block_ref[0, rows], block, (((1,), (1,)), ((), ())), preferred_element_type=F32)
    ln_ref[0, 0, 0] = STAT_DECAY * ls_ref[0, 0, 0] + (1.0 - STAT_DECAY) * left
    right = lax.dot_general(block_ref[0, :, rows], block, (((0,), (0,)), ((), ())), preferred_element_type=F32)
    rn_ref[0, 0, 0] = STAT_DECAY * rs_ref[0, 0, 0] + (1.0 - STAT_DECAY) * right


def grams(owned, left_stats, right_stats):
    part = pl.BlockSpec((1, 1, 1, TILE, BLK), lambda s, i: (0, 0, s, i, 0))
    return pl.pallas_call(
        grams_kernel,
        grid=(CAP, BLK // TILE),
        in_specs=[pl.BlockSpec((1, BLK, BLK), lambda s, i: (s, 0, 0)), part, part],
        out_specs=(part, part),
        out_shape=(
            jax.ShapeDtypeStruct(left_stats.shape, F32),
            jax.ShapeDtypeStruct(right_stats.shape, F32),
        ),
        compiler_params=pltpu.CompilerParams(vmem_limit_bytes=62 << 20),
        name="grams",
    )(owned, left_stats, right_stats)


def body(acts, grads_out, owners, left_stats, right_stats, left_root, right_root):
    owned, update = gradient_blocks(owners.reshape(-1), acts, grads_out, left_root, right_root)
    left_new, right_new = grams(owned, left_stats, right_stats)
    return (left_new, right_new, update)


def solution(mesh):
    placed = (
        P("dp", "group"),
        P("dp", "group"),
        P("dp", None, None),
        P("dp", "group", None, None, None),
        P("dp", "group", None, None, None),
        P("dp", "group", None, None, None),
        P("dp", "group", None, None, None),
    )
    return jax.shard_map(
        body,
        mesh=mesh,
        in_specs=placed,
        out_specs=(
            P("dp", "group", None, None, None),
            P("dp", "group", None, None, None),
            P(("group", "dp"), None, None),
        ),
        check_vma=False,
    )
```

```python
import functools

import jax
import jax.numpy as jnp
from jax import lax
from jax.experimental import pallas as pl
from jax.experimental.pallas import tpu as pltpu
from jax.sharding import PartitionSpec as P

MESH = pl.DeviceIdType.MESH
STAT_DECAY = 0.9
EPSILON = 1e-06
BLK = 512
HALF = BLK // 2
SIDE = 4
GROUPS = 8
CAP = 3
QUARTER = HALF // 2
COLS = 128
PER_HALF = BLK // COLS
ROUNDS = 2 * PER_HALF
SLOTS = 3
LAST_LAG = 3
F32 = jnp.float32
BF16 = jnp.bfloat16


def place():
    dp, group = lax.axis_index("dp"), lax.axis_index("group")
    return dp // SIDE, group // 2, lax.rem(dp, SIDE), lax.rem(group, 2)


def ring(index, step):
    return lax.rem(index + step + SIDE, SIDE)


def device(x, y, z, core):
    return (x * SIDE + z, y * 2 + core)


def remote(src, dst, send, recv, target):
    return pltpu.make_async_remote_copy(
        src_ref=src, dst_ref=dst, send_sem=send, recv_sem=recv, device_id=target, device_id_type=MESH
    )


def greet(targets):
    barrier = pltpu.get_barrier_semaphore()
    for target in targets:
        pl.semaphore_signal(barrier, inc=1, device_id=target, device_id_type=MESH)
    pl.semaphore_wait(barrier, len(targets))


def plus(*terms):
    total = terms[0].astype(F32)
    for term in terms[1:]:
        total = total + term.astype(F32)
    return total.astype(BF16)


class RingSum:
    def __init__(self, parts, me, right, left, far, near, send, recv):
        self.parts, self.me, self.far, self.near = parts, me, far, near

        def copy(d, half, dst, recv_sem, target):
            return remote(parts.at[ring(me, d), half], dst, send, recv_sem, target)

        self.copies = [
            copy(2, 0, far.at[0], recv.at[0], right),
            copy(2, 1, far.at[1], recv.at[1], left),
            copy(1, 1, near.at[0, 1], recv.at[2], right),
            copy(-1, 0, near.at[1, 0], recv.at[2], left),
            copy(1, 0, near.at[0, 0], recv.at[2], right),
            copy(-1, 1, near.at[1, 1], recv.at[2], left),
        ]
        sent = parts.at[pl.ds(0, SIDE - 1)]
        self.all_sent = remote(sent, sent, send, recv.at[2], right)
        self.all_near = remote(near, near, send, recv.at[2], right)

    def first(self):
        for copy in self.copies[:4]:
            copy.start()

    def merge(self):
        for j, (step, half) in enumerate(((1, 0), (-1, 1))):
            self.copies[j].wait_recv()
            at = ring(self.me, step)
            self.parts[at, half] = plus(self.parts[at, half], self.far[j])
            self.copies[4 + j].start()

    def total(self):
        self.all_near.wait_recv()
        return [plus(self.parts[self.me, half], self.near[0, half], self.near[1, half]) for half in range(2)]

    def finish(self):
        self.all_sent.wait_send()


class Routed:
    def __init__(self, parity, owners, table, y, core, along_y, here, there, packed, far, near, send, recv):
        self.parity, self.owners, self.table, self.y, self.core = parity, owners, table, y, core
        self.here, self.there, self.packed, self.far, self.near = here, there, packed, far, near
        self.order = (((2, 0), (2, 1)), ((1, 1), (-1, 0)), ((1, 0), (-1, 1)))
        landing = ((far.at[0], far.at[1]), (near.at[0, 1], near.at[1, 0]), (near.at[0, 0], near.at[1, 1]))
        self.copies = [
            remote(packed.at[i, j], landing[i][j], send, recv.at[j if i == 0 else 2], along_y[j])
            for i in range(3)
            for j in range(2)
        ]
        self.all_sent = remote(packed, packed, send, recv.at[2], along_y[0])
        self.all_near = remote(near, near, send, recv.at[2], along_y[0])

    def mine(self, step, half):
        k = 2 * (2 * ring(self.y, step) + self.core) + self.parity
        owner, at = self.owners[k], self.table[k]
        rows = pl.ds(half * HALF, HALF)
        return jnp.where(lax.rem(owner, 2) == self.core, self.here[at, rows], self.there[at, rows]), owner // 2

    def send(self, i):
        for j in range(2):
            self.packed[i, j] = self.mine(*self.order[i][j])[0]
            self.copies[2 * i + j].start()

    def merge(self):
        for j in range(2):
            self.copies[j].wait_recv()
            value, at = self.mine(*self.order[2][j])
            self.packed[2, j] = jnp.where(at == self.y, value, self.far[j])
            self.copies[4 + j].start()

    def last(self, out):
        self.all_near.wait_recv()
        for half in range(2):
            value, at = self.mine(0, half)
            from_left = at == ring(self.y, -1)
            if half == 0:
                from_left = from_left | (at == ring(self.y, 2))
            arrived = jnp.where(from_left, self.near[0, half], self.near[1, half])
            out[half * HALF : (half + 1) * HALF] = jnp.where(at == self.y, value, arrived)

    def finish(self):
        self.all_sent.wait_send()


def gradient_kernel(
    owners, acts_ref, grads_ref, lr_ref, rr_ref,
    owned_ref, out_ref,
    grads, turned, acts, parts, far1, near1, sums, far2, near2,
    roots, pair_roots, roots_packed, roots_far, roots_near, holder_roots,
    result, held, packed, back_far, back_near, owned, shaped, slot_table, rank_table, mine_table,
    local_sem, pair_send, pair_recv, acts_send, acts_recv, acts_cross_send, acts_cross_recv,
    send1, recv1, send2, recv2, out_send, out_recv, cross_send, cross_recv,
    roots_swap_send, roots_swap_recv, roots_send, roots_recv, swap_send, swap_recv, back_send, back_recv, owned_sem,
    *blocks,
):
    x, y, z, core = place()
    group = y * 2 + core
    partner = device(x, y, z, 1 - core)
    along_y = [device(x, ring(y, s), z, core) for s in (1, -1)]
    along_x = [device(ring(x, s), y, z, core) for s in (1, -1)]
    along_z = [device(x, y, ring(z, s), core) for s in (1, -1)]
    started = []

    def go(copy):
        copy.start()
        started.append(copy)
        return copy

    load_acts = [
        pltpu.make_async_copy(acts_ref.at[:, pl.ds(v * COLS, COLS)], acts.at[core, v, y], local_sem.at[v])
        for v in range(PER_HALF)
    ]
    load_grads = pltpu.make_async_copy(grads_ref, grads, local_sem.at[PER_HALF])
    load_roots = [
        pltpu.make_async_copy(ref.at[0, 0], roots.at[i], local_sem.at[PER_HALF + 1 + i])
        for i, ref in enumerate((lr_ref, rr_ref))
    ]
    for copy in load_acts + [load_grads] + load_roots:
        copy.start()
    greet([partner] + along_y + along_x + along_z)

    for copy in load_acts:
        copy.wait()
    own = acts.at[core, :, y]
    pair = go(remote(own, own, pair_send.at[0], pair_recv.at[0], partner))
    spans = ((0, 0, 1), (0, 1, PER_HALF - 1), (1, 0, PER_HALF))
    gathers, gather_crosses = {}, {}

    def tokens(g, at, start, size):
        h, first, number = spans[g]
        return acts.at[h, pl.ds(first, number), at, pl.ds(pl.multiple_of(core * HALF + start, 16), size)]

    def acts_first(g):
        gathers[g], gather_crosses[g] = [], []
        for i in range(2):
            for j in range(2):
                here, n = tokens(g, y, (i ^ j) * QUARTER, QUARTER), 2 * i + j
                gathers[g].append(go(remote(here, here, acts_send.at[g, n], acts_recv.at[g, n], along_y[j])))

    def acts_cross(g, i, at):
        here = tokens(g, at, 0, HALF)
        gather_crosses[g].append(
            go(remote(here, here, acts_cross_send.at[g, i], acts_cross_recv.at[g, i], partner))
        )

    def acts_forward(g):
        for j in range(2):
            gathers[g][j].wait_recv()
            here, n = tokens(g, ring(y, (-1, 1)[j]), j * QUARTER, QUARTER), 4 + j
            gathers[g].append(go(remote(here, here, acts_send.at[g, n], acts_recv.at[g, n], along_y[j])))
        for j in range(2):
            gathers[g][2 + j].wait_recv()
            acts_cross(g, j, ring(y, (-1, 1)[j]))

    def acts_last(g):
        for copy in gathers[g][4:]:
            copy.wait_recv()
        acts_cross(g, 2, ring(y, 2))

    def acts_ready(g):
        for copy in gather_crosses[g]:
            copy.wait_recv()

    pair.wait_recv()
    acts_first(0)
    acts_first(1)

    count = 2 * GROUPS
    owner = [owners[k] for k in range(count)]
    zero, one = jnp.int32(0), jnp.int32(1)
    slot, rank = [], []
    for k in range(count):
        same = [jnp.where(owner[k2] == owner[k], one, zero) for k2 in range(k)]
        slot.append(sum(same, zero))
        rank.append(sum(same[0::2], zero))
        slot_table[k] = jnp.minimum(slot[k], CAP - 1)
        rank_table[k] = jnp.minimum(rank[k], CAP - 1)
    is_mine = [owner[k] == group for k in range(count)]

    def pick(positions, test, value):
        return sum([jnp.where(is_mine[k] & test(k), value(k), zero) for k in positions], zero)

    for j in range(CAP):
        even, test = range(0, count, 2), lambda k, j=j: rank[k] == j
        mine_table[3 * j] = pick(even, test, lambda k: jnp.int32(k // 2 % 2))
        mine_table[3 * j + 1] = pick(even, test, lambda k: jnp.int32(k // 4))
        mine_table[3 * j + 2] = pick(even, test, lambda k: jnp.minimum(slot[k], CAP - 1))
        every, test, at = range(count), lambda k, j=j: slot[k] == j, 3 * CAP + 4 * j
        mine_table[at] = pick(every, test, lambda k: jnp.int32(k % 2))
        mine_table[at + 1] = pick(every, test, lambda k: one)
        mine_table[at + 2] = pick(every, test, lambda k: jnp.int32(k // 2 % 2))
        mine_table[at + 3] = pick(every, test, lambda k: jnp.int32(k // 4))

    load_grads.wait()
    for xd in range(SIDE):
        for start in range(0, BLK, QUARTER):
            turned[xd, start : start + QUARTER, :] = grads[:, xd * BLK + start : xd * BLK + start + QUARTER].T
    acts_forward(0)
    for copy in load_roots:
        copy.wait()
    acts_last(0)
    roots_swap = go(remote(roots, pair_roots, roots_swap_send.at[0], roots_swap_recv.at[0], partner))

    stages1, stages2, outs, crosses = {}, {}, {}, {}

    def products(r):
        p, v, b = r // PER_HALF, r % PER_HALF, r % SLOTS
        if r < 2:
            acts_ready(r)
        if r == PER_HALF:
            acts_ready(2)
        right = jnp.concatenate([acts[p, v, zd] for zd in range(SIDE)], axis=1)
        for u in range(2):
            if r >= SLOTS:
                stages1[r - SLOTS, u].finish()

            left = turned[:, u * HALF : (u + 1) * HALF].reshape(SIDE * HALF, BLK)
            value = jnp.dot(left, right, preferred_element_type=F32).astype(BF16)
            for xd in range(SIDE):
                for half in range(2):
                    rows = value[xd * HALF + half * QUARTER : xd * HALF + (half + 1) * QUARTER]
                    if u == 0:
                        parts[b, 0, xd, half] = rows
                    else:
                        for zd in range(SIDE):
                            lanes = slice(zd * COLS, (zd + 1) * COLS)
                            parts[b, 1, zd, half, :, xd * COLS : (xd + 1) * COLS] = rows[:, lanes]
            me, (right_to, left_to) = ((x, along_x), (z, along_z))[u]
            stage = RingSum(
                parts.at[b, u], me, right_to, left_to, far1.at[b, u], near1.at[b, u], send1.at[b, u], recv1.at[b, u]
            )
            stage.first()
            stages1[r, u] = stage

    def merge1(r):
        for u in range(2):
            stages1[r, u].merge()

    def between(r):
        b = r % SLOTS
        for u in range(2):
            if r >= SLOTS:
                stages2[r - SLOTS, u].finish()
            total = stages1[r, u].total()
            for half in range(2):
                for d in range(SIDE):
                    sums[b, u, d, half] = total[half][:, d * COLS : (d + 1) * COLS]
            me, (right_to, left_to) = ((z, along_z), (x, along_x))[u]
            stage = RingSum(
                sums.at[b, u], me, right_to, left_to, far2.at[b, u], near2.at[b, u], send2.at[b, u], recv2.at[b, u]
            )
            stage.first()
            stages2[r, u] = stage

    def merge2(r):
        for u in range(2):
            stages2[r, u].merge()

    def strip(r, at, half):
        return blocks[r].at[core, at, pl.ds(half * HALF, HALF)]

    def spread(r):
        for u in range(2):
            total = stages2[r, u].total()
            for half in range(2):
                start = u * HALF + half * QUARTER
                blocks[r][core, y, start : start + QUARTER] = total[half]
        outs[r] = []
        for i in range(2):
            for j in range(2):
                here = strip(r, y, i ^ j)
                outs[r].append(remote(here, here, out_send.at[r], out_recv.at[r, 2 * i + j], along_y[j]))
                outs[r][-1].start()

    def pass_on(r):
        for j in range(2):
            outs[r][j].wait_recv()
            here = strip(r, ring(y, (-1, 1)[j]), j)
            outs[r].append(remote(here, here, out_send.at[r], out_recv.at[r, 4 + j], along_y[j]))
            outs[r][-1].start()

    def pass_last(r):
        for copy in outs[r][2:]:
            copy.wait_recv()
        here = blocks[r].at[core]
        crosses[r] = go(remote(here, here, cross_send.at[r], cross_recv.at[r], partner))

    def spread_finish(r):
        sent = blocks[r].at[core, pl.ds(0, SIDE - 1)]
        remote(sent, sent, out_send.at[r], out_recv.at[r, 0], partner).wait_send()

    def condition(shaped_block, right_root):
        product = jnp.dot(shaped_block, right_root, preferred_element_type=F32)
        scaling = lax.rsqrt(jnp.mean(product * product) + EPSILON)
        return (product * scaling).astype(BF16)

    swaps = []

    def shape_part(v):
        for j in range(CAP):
            c, to, at = [mine_table[3 * j + i] for i in range(3)]
            pair_of = jnp.concatenate([blocks[v][c, to], blocks[v + 1][c, to]], axis=1)
            value = jnp.dot(roots[0, at], pair_of, preferred_element_type=F32)
            shaped[j, :, v * COLS : (v + 2) * COLS] = value.astype(BF16)

    def precondition():
        for j in range(CAP):
            result[j] = condition(shaped[j], roots[1, mine_table[3 * j + 2]])
            swaps.append(go(remote(result.at[j], held.at[j], swap_send.at[j], swap_recv.at[j], partner)))

    back = Routed(
        0, owners, rank_table, y, core, along_y, result, held, packed, back_far, back_near, back_send.at[0], back_recv
    )
    left1, right1 = [
        Routed(
            1, owners, slot_table, y, core, along_y, roots.at[n], pair_roots.at[n],
            roots_packed.at[n], roots_far.at[n], roots_near.at[n], roots_send.at[n], roots_recv.at[n],
        )
        for n in range(2)
    ]

    def collect(r):
        p, cols = r // PER_HALF, slice(r % PER_HALF * COLS, (r % PER_HALF + 1) * COLS)
        for s in range(CAP):
            odd, used, c, at = [mine_table[3 * CAP + 4 * s + i] for i in range(4)]
            value = blocks[r][c, at]
            if p == 0:
                owned[s, :, cols] = jnp.where((used > 0) & (odd == 0), value, jnp.zeros_like(value))
            else:
                owned[s, :, cols] = jnp.where(odd > 0, value, owned[s, :, cols])

    def at_lag(part, lag):
        if 0 <= step - lag < ROUNDS:
            part(step - lag)

    half_done = PER_HALF - 1 + LAST_LAG
    for step in range(ROUNDS + 4):
        at_lag(products, 0)
        at_lag(spread, 2)
        if step == half_done and LAST_LAG < 4:
            pass_last(PER_HALF - 2)
            pass_last(PER_HALF - 1)
        elif step not in (half_done, half_done + 1) or LAST_LAG == 4:
            at_lag(pass_last, 4)
        if step == half_done:
            crosses[2].wait_recv()
            crosses[3].wait_recv()
            shape_part(2)
            precondition()
        at_lag(between, 1)
        at_lag(merge1, 0)
        at_lag(merge2, 1)
        if step == half_done - 1:
            crosses[0].wait_recv()
            crosses[1].wait_recv()
            shape_part(0)
        if LAST_LAG < 4 and step == half_done - 1:
            pass_on(PER_HALF - 2)
            pass_on(PER_HALF - 1)
        elif LAST_LAG == 4 or step != half_done:
            at_lag(pass_on, 3)
        if step == 0:
            acts_forward(1)
            roots_swap.wait_recv()
            left1.send(0)
            acts_last(1)
        if step == 1:
            acts_first(2)
            left1.send(1)
        if step == 2:
            acts_forward(2)
            left1.merge()
        if step == 3:
            acts_last(2)
            right1.send(0)
        if step == 4:
            right1.send(1)
        if step == 5:
            right1.merge()
        if step == half_done:
            for copy in swaps:
                copy.wait_recv()
            back.send(0)
            back.send(1)
        if step == half_done + 1:
            back.merge()
        if step == 8:
            left1.last(holder_roots.at[0])
            right1.last(holder_roots.at[1])
            for r in range(PER_HALF):
                collect(r)
        if step == 9:
            block = jnp.concatenate([blocks[PER_HALF + v][core, y] for v in range(PER_HALF)], axis=1)
            block = jnp.dot(holder_roots[0], block, preferred_element_type=F32).astype(BF16)
            out_ref[1] = condition(block, holder_roots[1])
        if step == 10:
            back.last(out_ref.at[0])
        if step >= 9:
            crosses[step - 5].wait_recv()
            collect(step - 5)
    crosses[ROUNDS - 1].wait_recv()
    collect(ROUNDS - 1)
    kept = []
    for s in range(CAP):
        kept.append(pltpu.make_async_copy(owned.at[s], owned_ref.at[s], owned_sem.at[s]))
        kept[s].start()

    for copy in started:
        copy.wait_send()
    for part in (left1, right1, back):
        part.finish()
    for r in range(ROUNDS):
        spread_finish(r)
    for r in range(ROUNDS - SLOTS, ROUNDS):
        for u in range(2):
            stages1[r, u].finish()
            stages2[r, u].finish()
    for copy in kept:
        copy.wait()


def gradient_blocks(owners, acts, grads_out, left_root, right_root):
    dma = pltpu.SemaphoreType.DMA
    square, half, wide, small = (BLK, BLK), (HALF, BLK), (QUARTER, BLK), (QUARTER, COLS)
    shapes = [
        (BLK, SIDE * BLK),
        (SIDE,) + square,
        (2, PER_HALF, SIDE, BLK, COLS),
        (SLOTS, 2, SIDE, 2) + wide,
        (SLOTS, 2, 2) + wide,
        (SLOTS, 2, 2, 2) + wide,
        (SLOTS, 2, SIDE, 2) + small,
        (SLOTS, 2, 2) + small,
        (SLOTS, 2, 2, 2) + small,
        (2, CAP) + square,
        (2, CAP) + square,
        (2, 3, 2) + half,
        (2, 2) + half,
        (2, 2, 2) + half,
        (2,) + square,
        (CAP,) + square,
        (CAP,) + square,
        (3, 2) + half,
        (2,) + half,
        (2, 2) + half,
        (CAP,) + square,
        (CAP,) + square,
    ]
    semaphores = [
        (PER_HALF + 3,), (1,), (1,), (3, 6), (3, 6), (3, 3), (3, 3),
        (SLOTS, 2), (SLOTS, 2, 3), (SLOTS, 2), (SLOTS, 2, 3),
        (ROUNDS,), (ROUNDS, 6), (ROUNDS,), (ROUNDS,),
        (1,), (1,), (2,), (2, 3), (CAP,), (CAP,), (1,), (3,), (CAP,),
    ]
    return pl.pallas_call(
        gradient_kernel,
        out_shape=(
            jax.ShapeDtypeStruct((CAP, BLK, BLK), BF16),
            jax.ShapeDtypeStruct((2, BLK, BLK), BF16),
        ),
        in_specs=[pl.BlockSpec(memory_space=pltpu.SMEM)] + [pl.BlockSpec(memory_space=pl.ANY)] * 4,
        out_specs=(pl.BlockSpec(memory_space=pl.ANY), pl.BlockSpec(memory_space=pltpu.VMEM)),
        scratch_shapes=[pltpu.VMEM(shape, BF16) for shape in shapes]
        + [pltpu.SMEM((2 * GROUPS,), jnp.int32)] * 2
        + [pltpu.SMEM((7 * CAP,), jnp.int32)]
        + [dma(shape) for shape in semaphores]
        + [pltpu.VMEM((2, SIDE, BLK, COLS), BF16)] * ROUNDS,
        compiler_params=pltpu.CompilerParams(
            collective_id=0, has_side_effects=True, vmem_limit_bytes=62 << 20
        ),
        cost_estimate=pl.CostEstimate(flops=12 << 30, bytes_accessed=10 << 20, transcendentals=0),
        name="gradient_blocks",
    )(owners, acts, grads_out, left_root, right_root)


def grams_kernel(
    owned_ref, ls_ref, rs_ref, held_ref, ln_ref, rn_ref, out_ref, owned, left_stats, right_stats, held, load_sem, store_sem, held_sem
):
    loads = [
        [
            pltpu.make_async_copy(ls_ref.at[0, 0, s], left_stats.at[s], load_sem.at[s, 0]),
            pltpu.make_async_copy(rs_ref.at[0, 0, s], right_stats.at[s], load_sem.at[s, 1]),
            pltpu.make_async_copy(owned_ref.at[s], owned.at[s], load_sem.at[s, 2]),
        ]
        for s in range(CAP)
    ]
    for copies in loads:
        for copy in copies:
            copy.start()
    load_held = pltpu.make_async_copy(held_ref, held, held_sem.at[0])
    load_held.start()
    stores = [pltpu.make_async_copy(held, out_ref, held_sem.at[1])]
    for s in range(CAP):
        for copy in loads[s]:
            copy.wait()
        block = owned[s]
        sides = ((left_stats, ln_ref, 1), (right_stats, rn_ref, 0))
        for i, (stats, new_ref, dim) in enumerate(sides):
            gram = lax.dot_general(block, block, (((dim,), (dim,)), ((), ())), preferred_element_type=F32)
            stats[s] = STAT_DECAY * stats[s] + (1.0 - STAT_DECAY) * gram
            store = pltpu.make_async_copy(stats.at[s], new_ref.at[0, 0, s], store_sem.at[s, i])
            store.start()
            stores.append(store)
        if s == CAP - 2:
            load_held.wait()
            stores[0].start()
    for store in stores:
        store.wait()


def grams(owned, left_stats, right_stats, update):
    dma = pltpu.SemaphoreType.DMA
    return pl.pallas_call(
        grams_kernel,
        in_specs=[pl.BlockSpec(memory_space=pl.ANY)] * 4,
        out_specs=[pl.BlockSpec(memory_space=pl.ANY)] * 3,
        out_shape=(
            jax.ShapeDtypeStruct(left_stats.shape, F32),
            jax.ShapeDtypeStruct(right_stats.shape, F32),
            jax.ShapeDtypeStruct(update.shape, BF16),
        ),
        scratch_shapes=[
            pltpu.VMEM((CAP, BLK, BLK), BF16),
            pltpu.VMEM((CAP, BLK, BLK), F32),
            pltpu.VMEM((CAP, BLK, BLK), F32),
            pltpu.VMEM(update.shape, BF16),
            dma((CAP, 3)), dma((CAP, 2)), dma((2,)),
        ],
        compiler_params=pltpu.CompilerParams(vmem_limit_bytes=62 << 20),
        name="grams",
    )(owned, left_stats, right_stats, update)


def body(acts, grads_out, owners, left_stats, right_stats, left_root, right_root):
    owned, update = gradient_blocks(owners.reshape(-1), acts, grads_out, left_root, right_root)
    return grams(owned, left_stats, right_stats, update)


def solution(mesh):
    placed = (
        P("dp", "group"),
        P("dp", "group"),
        P("dp", None, None),
        P("dp", "group", None, None, None),
        P("dp", "group", None, None, None),
        P("dp", "group", None, None, None),
        P("dp", "group", None, None, None),
    )
    return jax.shard_map(
        body,
        mesh=mesh,
        in_specs=placed,
        out_specs=(
            P("dp", "group", None, None, None),
            P("dp", "group", None, None, None),
            P(("group", "dp"), None, None),
        ),
        check_vma=False,
    )
```

```python
import functools

import jax
import jax.numpy as jnp
from jax import lax
from jax.experimental import pallas as pl
from jax.experimental.pallas import tpu as pltpu
from jax.sharding import PartitionSpec as P

MESH = pl.DeviceIdType.MESH
STAT_DECAY = 0.9
EPSILON = 1e-06
BLK = 512
HALF = BLK // 2
SIDE = 4
GROUPS = 8
CAP = 3
QUARTER = HALF // 2
SIZES = (64, 64, 64, 64, 64, 64, 64, 64)
ROUNDS = len(SIZES)
PER_HALF = ROUNDS // 2
LARGEST = max(SIZES)
STARTS = [2 * sum(SIZES[r - r % PER_HALF : r]) for r in range(ROUNDS)]
SLOTS = 3
MERGE1, BETWEEN, MERGE2, SPREAD, PASS_ON, PASS_LAST = 0, 1, 1, 2, 2, 3
F32 = jnp.float32
BF16 = jnp.bfloat16


def place():
    dp, group = lax.axis_index("dp"), lax.axis_index("group")
    return dp // SIDE, group // 2, lax.rem(dp, SIDE), lax.rem(group, 2)


def ring(index, step):
    return lax.rem(index + step + SIDE, SIDE)


def device(x, y, z, core):
    return (x * SIDE + z, y * 2 + core)


def remote(src, dst, send, recv, target):
    return pltpu.make_async_remote_copy(
        src_ref=src, dst_ref=dst, send_sem=send, recv_sem=recv, device_id=target, device_id_type=MESH
    )


def greet(targets):
    barrier = pltpu.get_barrier_semaphore()
    for target in targets:
        pl.semaphore_signal(barrier, inc=1, device_id=target, device_id_type=MESH)
    pl.semaphore_wait(barrier, len(targets))


def plus(*terms):
    total = terms[0].astype(F32)
    for term in terms[1:]:
        total = total + term.astype(F32)
    return total.astype(BF16)


class RingSum:
    def __init__(self, parts, me, right, left, far, near, send, recv):
        self.parts, self.me, self.far, self.near = parts, me, far, near

        def copy(d, half, dst, recv_sem, target):
            return remote(parts.at[ring(me, d), half], dst, send, recv_sem, target)

        self.copies = [
            copy(2, 0, far.at[0], recv.at[0], right),
            copy(2, 1, far.at[1], recv.at[1], left),
            copy(1, 1, near.at[0, 1], recv.at[2], right),
            copy(-1, 0, near.at[1, 0], recv.at[2], left),
            copy(1, 0, near.at[0, 0], recv.at[2], right),
            copy(-1, 1, near.at[1, 1], recv.at[2], left),
        ]
        sent = parts.at[pl.ds(0, SIDE - 1)]
        self.all_sent = remote(sent, sent, send, recv.at[2], right)
        self.all_near = remote(near, near, send, recv.at[2], right)

    def first(self):
        for copy in self.copies[:4]:
            copy.start()

    def merge(self):
        for j, (step, half) in enumerate(((1, 0), (-1, 1))):
            self.copies[j].wait_recv()
            at = ring(self.me, step)
            self.parts[at, half] = plus(self.parts[at, half], self.far[j])
            self.copies[4 + j].start()

    def total(self):
        self.all_near.wait_recv()
        return [plus(self.parts[self.me, half], self.near[0, half], self.near[1, half]) for half in range(2)]

    def finish(self):
        self.all_sent.wait_send()


def gradient_kernel(
    owners, acts_ref, grads_ref, lr_ref, rr_ref,
    owned_ref, out_ref,
    grads, turned, acts, parts, far1, near1, sums, far2, near2, blocks0, blocks1,
    roots, pair_roots, roots_packed, roots_far, roots_near, holder_roots,
    result, held, packed, back_far, back_near, owned, slot_table, rank_table,
    local_sem, pair_send, pair_recv, acts_send, acts_recv, acts_cross_send, acts_cross_recv,
    send1, recv1, send2, recv2, out_send, out_recv, cross_send, cross_recv,
    swap_send, swap_recv, back_send, back_recv, roots_swap_send, roots_swap_recv, roots_send, roots_recv, owned_sem,
):
    x, y, z, core = place()
    group = y * 2 + core
    partner = device(x, y, z, 1 - core)
    along_y = [device(x, ring(y, s), z, core) for s in (1, -1)]
    along_x = [device(ring(x, s), y, z, core) for s in (1, -1)]
    along_z = [device(x, y, ring(z, s), core) for s in (1, -1)]
    blocks = (blocks0, blocks1)
    started = []

    def go(copy):
        copy.start()
        started.append(copy)
        return copy

    load_acts = pltpu.make_async_copy(acts_ref, acts.at[core, y], local_sem.at[0])
    load_grads = pltpu.make_async_copy(grads_ref, grads, local_sem.at[1])
    load_roots = [
        pltpu.make_async_copy(ref.at[0, 0], roots.at[i], local_sem.at[2 + i]) for i, ref in enumerate((lr_ref, rr_ref))
    ]
    load_acts.start()
    load_grads.start()
    for copy in load_roots:
        copy.start()
    greet([partner] + along_y + along_x + along_z)

    load_acts.wait()
    own = acts.at[core, y]
    pair = go(remote(own, own, pair_send.at[0], pair_recv.at[0], partner))
    gathers = {}

    def rows_of(h, at, start, size):
        return acts.at[h, at, pl.ds(pl.multiple_of(core * HALF + start, 16), size)]

    def acts_first(h):
        gathers[h] = []
        for i in range(2):
            for j in range(2):
                here = rows_of(h, y, (i ^ j) * QUARTER, QUARTER)
                n = 2 * i + j
                gathers[h].append(go(remote(here, here, acts_send.at[h, n], acts_recv.at[h, n], along_y[j])))
        gathers[h, "cross"] = []

    def acts_cross(h, i, at):
        here = rows_of(h, at, 0, HALF)
        gathers[h, "cross"].append(
            go(remote(here, here, acts_cross_send.at[h, i], acts_cross_recv.at[h, i], partner))
        )

    def acts_forward(h):
        for j in range(2):
            gathers[h][j].wait_recv()
            here = rows_of(h, ring(y, (-1, 1)[j]), j * QUARTER, QUARTER)
            n = 4 + j
            gathers[h].append(go(remote(here, here, acts_send.at[h, n], acts_recv.at[h, n], along_y[j])))
        for j in range(2):
            gathers[h][2 + j].wait_recv()
            acts_cross(h, j, ring(y, (-1, 1)[j]))

    def acts_last(h):
        for copy in gathers[h][4:]:
            copy.wait_recv()
        acts_cross(h, 2, ring(y, 2))

    def acts_ready(h):
        for copy in gathers[h, "cross"]:
            copy.wait_recv()

    pair.wait_recv()
    acts_first(0)

    count = 2 * GROUPS
    owner = [owners[k] for k in range(count)]
    zero, one = jnp.int32(0), jnp.int32(1)
    slot, rank = [], []
    for k in range(count):
        same = [jnp.where(owner[k2] == owner[k], one, zero) for k2 in range(k)]
        slot.append(sum(same, zero))
        rank.append(sum(same[0::2], zero))
        slot_table[k] = jnp.minimum(slot[k], CAP - 1)
        rank_table[k] = jnp.minimum(rank[k], CAP - 1)
    is_mine = [owner[k] == group for k in range(count)]

    def pick(positions, test, value):
        return sum([jnp.where(is_mine[k] & test(k), value(k), zero) for k in positions], zero)

    load_grads.wait()
    for xd in range(SIDE):
        for start in range(0, BLK, QUARTER):
            turned[xd, start : start + QUARTER, :] = grads[:, xd * BLK + start : xd * BLK + start + QUARTER].T
    acts_forward(0)
    for copy in load_roots:
        copy.wait()
    acts_last(0)
    roots_swap = go(remote(roots, pair_roots, roots_swap_send.at[0], roots_swap_recv.at[0], partner))

    stages1, stages2, outs, crosses = {}, {}, {}, {}

    def products(r):
        p, b, size = r // PER_HALF, r % SLOTS, SIZES[r]
        if r % PER_HALF == 0:
            acts_ready(p)
        for u in range(2):
            if r >= SLOTS:
                stages1[r - SLOTS, u].finish()
            left = turned[:, STARTS[r] + u * size : STARTS[r] + (u + 1) * size, :].reshape(SIDE * size, BLK)

            def step(zd, carry, u=u, left=left):
                value = jnp.dot(left, acts[p, zd], preferred_element_type=F32).astype(BF16)
                for xd in range(SIDE):
                    piece = value[xd * size : (xd + 1) * size]
                    if u == 0:
                        parts[b, 0, xd, zd // 2, lax.rem(zd, 2), 0:size] = piece
                    else:
                        parts[b, 1, zd, xd // 2, xd % 2, 0:size] = piece
                return carry

            lax.fori_loop(0, SIDE, step, 0)
            me, (right, left_to) = ((x, along_x), (z, along_z))[u]
            stage = RingSum(
                parts.at[b, u], me, right, left_to, far1.at[b, u], near1.at[b, u], send1.at[b, u], recv1.at[b, u]
            )
            stage.first()
            stages1[r, u] = stage

    def merge1(r):
        for u in range(2):
            stages1[r, u].merge()

    def between(r):
        b, size = r % SLOTS, SIZES[r] // 2
        for u in range(2):
            if r >= SLOTS:
                stages2[r - SLOTS, u].finish()
            total = stages1[r, u].total()
            for half in range(2):
                for o in range(2):
                    for piece in range(2):
                        sums[b, u, half * 2 + o, piece, 0:size] = total[half][o, piece * size : (piece + 1) * size]
            me, (right, left_to) = ((z, along_z), (x, along_x))[u]
            stage = RingSum(
                sums.at[b, u], me, right, left_to, far2.at[b, u], near2.at[b, u], send2.at[b, u], recv2.at[b, u]
            )
            stage.first()
            stages2[r, u] = stage

    def merge2(r):
        for u in range(2):
            stages2[r, u].merge()

    def strip(r, at, start, size):
        return blocks[r // PER_HALF].at[at, pl.ds(STARTS[r] + start, size)]

    def cross(r, i, at):
        here = strip(r, at, 0, 2 * SIZES[r])
        crosses[r].append(go(remote(here, here, cross_send.at[r, i], cross_recv.at[r, i], partner)))

    def spread(r):
        p, size = r // PER_HALF, SIZES[r]
        for u in range(2):
            total = stages2[r, u].total()
            for half in range(2):
                start = STARTS[r] + u * size + half * (size // 2)
                blocks[p][group, start : start + size // 2] = total[half]
        outs[r], crosses[r] = [], []
        for i in range(2):
            for j in range(2):
                here, n = strip(r, group, (i ^ j) * size, size), 2 * i + j
                outs[r].append(go(remote(here, here, out_send.at[r, n], out_recv.at[r, n], along_y[j])))
        cross(r, 0, group)

    def pass_on(r):
        for j in range(2):
            outs[r][j].wait_recv()
            here, n = strip(r, 2 * ring(y, (-1, 1)[j]) + core, j * SIZES[r], SIZES[r]), 4 + j
            outs[r].append(go(remote(here, here, out_send.at[r, n], out_recv.at[r, n], along_y[j])))
        for j in range(2):
            outs[r][2 + j].wait_recv()
            cross(r, 1 + j, 2 * ring(y, (-1, 1)[j]) + core)

    def pass_last(r):
        for copy in outs[r][4:]:
            copy.wait_recv()
        cross(r, 3, 2 * ring(y, 2) + core)

    def blocks_ready(p):
        for r in range(p * PER_HALF, (p + 1) * PER_HALF):
            for copy in crosses[r]:
                copy.wait_recv()

    def condition(left_root, block, right_root):
        shaped = jnp.dot(left_root, block, preferred_element_type=F32).astype(BF16)
        product = jnp.dot(shaped, right_root, preferred_element_type=F32)
        scaling = lax.rsqrt(jnp.mean(product * product) + EPSILON)
        return (product * scaling).astype(BF16)

    swaps = []

    def precondition():
        for j in range(CAP):
            def test(k, j=j):
                return rank[k] == j

            even = range(0, count, 2)
            which, at = pick(even, test, lambda k: jnp.int32(k // 2)), pick(even, test, lambda k: jnp.minimum(slot[k], CAP - 1))
            result[j] = condition(roots[0, at], blocks0[which], roots[1, at])
            swaps.append(go(remote(result.at[j], held.at[j], swap_send.at[j], swap_recv.at[j], partner)))

    class Routed:
        def __init__(self, parity, table, sources, packed, far, near, send, recv):
            self.parity, self.table, self.sources = parity, table, sources
            self.packed, self.far, self.near = packed, far, near
            self.order = (((2, 0), (2, 1)), ((1, 1), (-1, 0)), ((1, 0), (-1, 1)))
            landing = ((far.at[0], far.at[1]), (near.at[0, 1], near.at[1, 0]), (near.at[0, 0], near.at[1, 1]))
            self.copies = [
                remote(packed.at[i, j], landing[i][j], send.at[2 * i + j], recv.at[2 * i + j], along_y[j])
                for i in range(3)
                for j in range(2)
            ]

        def mine(self, step, half):
            k = 2 * (2 * ring(y, step) + core) + self.parity
            owner, at = owners[k], self.table[k]
            rows = pl.ds(half * HALF, HALF)
            return [
                jnp.where(lax.rem(owner, 2) == core, here(at, rows), there(at, rows)) for here, there in self.sources
            ], owner // 2

        def send(self, i):
            for j in range(2):
                for n, value in enumerate(self.mine(*self.order[i][j])[0]):
                    self.packed[i, j, n] = value
                go(self.copies[2 * i + j])

        def merge(self):
            for j in range(2):
                self.copies[j].wait_recv()
                values, at = self.mine(*self.order[2][j])
                for n, value in enumerate(values):
                    self.packed[2, j, n] = jnp.where(at == y, value, self.far[j, n])
                go(self.copies[4 + j])

        def last(self, store):
            for copy in self.copies[2:]:
                copy.wait_recv()
            for half in range(2):
                values, at = self.mine(0, half)
                from_left = at == ring(y, -1)
                if half == 0:
                    from_left = from_left | (at == ring(y, 2))
                for n, value in enumerate(values):
                    arrived = jnp.where(from_left, self.near[0, half, n], self.near[1, half, n])
                    store(n, half, jnp.where(at == y, value, arrived))

    back = Routed(
        0, rank_table, [(lambda at, rows: result[at, rows], lambda at, rows: held[at, rows])],
        packed, back_far, back_near, back_send, back_recv,
    )
    routed = [
        Routed(
            1, slot_table,
            [(lambda at, rows, n=n: roots[n, at, rows], lambda at, rows, n=n: pair_roots[n, at, rows])],
            roots_packed.at[n], roots_far.at[n], roots_near.at[n], roots_send.at[n], roots_recv.at[n],
        )
        for n in range(2)
    ]

    def store_roots(side, _, half, value):
        holder_roots[side, half * HALF : (half + 1) * HALF] = value

    def store_update(n, half, value):
        out_ref[0, half * HALF : (half + 1) * HALF] = value

    def collect(s):
        def test(k):
            return slot[k] == s

        every = range(count)
        odd = pick(every, test, lambda k: jnp.int32(k % 2))
        at = pick(every, test, lambda k: jnp.int32(k // 2))
        used = pick(every, test, lambda k: one)
        block = jnp.where(odd > 0, blocks1[at], blocks0[at])
        owned[s] = jnp.where(used > 0, block, jnp.zeros_like(block))
        copy = pltpu.make_async_copy(owned.at[s], owned_ref.at[s], owned_sem.at[s])
        copy.start()
        return copy

    half_done = PER_HALF - 1 + PASS_LAST

    def at_lag(part, lag):
        if 0 <= step - lag < ROUNDS:
            part(step - lag)

    for step in range(ROUNDS + PASS_LAST):
        at_lag(products, 0)
        at_lag(spread, SPREAD)
        at_lag(pass_last, PASS_LAST)
        at_lag(between, BETWEEN)
        if step == half_done:
            blocks_ready(0)
            precondition()
        at_lag(merge1, MERGE1)
        at_lag(merge2, MERGE2)
        if step == ROUNDS - 1 + SPREAD:
            out_ref[1] = condition(holder_roots[0], blocks1[group], holder_roots[1])
        at_lag(pass_on, PASS_ON)
        if step == 0:
            acts_first(1)
            roots_swap.wait_recv()
            routed[0].send(0)
        if step == 1:
            acts_forward(1)
            routed[0].send(1)
        if step == 2:
            acts_last(1)
            routed[0].merge()
        if step == 3:
            routed[1].send(0)
        if step == 4:
            routed[1].send(1)
        if step == 5:
            routed[1].merge()
        if step == half_done:
            for copy in swaps:
                copy.wait_recv()
            back.send(0)
            back.send(1)
        if step == ROUNDS - 1:
            for n in range(2):
                routed[n].last(functools.partial(store_roots, n))
        if step == half_done + 1:
            back.merge()
    back.last(store_update)
    blocks_ready(1)
    kept = [collect(s) for s in range(CAP)]

    for copy in started:
        copy.wait_send()
    for r in range(ROUNDS - SLOTS, ROUNDS):
        for u in range(2):
            stages1[r, u].finish()
            stages2[r, u].finish()
    for copy in kept:
        copy.wait()


def gradient_blocks(owners, acts, grads_out, left_root, right_root):
    dma = pltpu.SemaphoreType.DMA
    piece, small, square, half = (2, LARGEST, BLK), (LARGEST // 2, BLK), (BLK, BLK), (HALF, BLK)
    shapes = [
        (BLK, SIDE * BLK),
        (SIDE,) + square,
        (2, SIDE) + square,
        (SLOTS, 2, SIDE, 2) + piece,
        (SLOTS, 2, 2) + piece,
        (SLOTS, 2, 2, 2) + piece,
        (SLOTS, 2, SIDE, 2) + small,
        (SLOTS, 2, 2) + small,
        (SLOTS, 2, 2, 2) + small,
        (GROUPS,) + square,
        (GROUPS,) + square,
        (2, CAP) + square,
        (2, CAP) + square,
        (2, 3, 2, 1) + half,
        (2, 2, 1) + half,
        (2, 2, 2, 1) + half,
        (2,) + square,
        (CAP,) + square,
        (CAP,) + square,
        (3, 2, 1) + half,
        (2, 1) + half,
        (2, 2, 1) + half,
        (CAP,) + square,
    ]
    semaphores = [
        (4,), (1,), (1,), (2, 6), (2, 6), (2, 3), (2, 3),
        (SLOTS, 2), (SLOTS, 2, 3), (SLOTS, 2), (SLOTS, 2, 3),
        (ROUNDS, 6), (ROUNDS, 6), (ROUNDS, 4), (ROUNDS, 4),
        (CAP,), (CAP,), (6,), (6,), (1,), (1,), (2, 6), (2, 6), (CAP,),
    ]
    return pl.pallas_call(
        gradient_kernel,
        out_shape=(
            jax.ShapeDtypeStruct((CAP, BLK, BLK), BF16),
            jax.ShapeDtypeStruct((2, BLK, BLK), BF16),
        ),
        in_specs=[pl.BlockSpec(memory_space=pltpu.SMEM)] + [pl.BlockSpec(memory_space=pl.ANY)] * 4,
        out_specs=(pl.BlockSpec(memory_space=pl.ANY), pl.BlockSpec(memory_space=pltpu.VMEM)),
        scratch_shapes=[pltpu.VMEM(shape, BF16) for shape in shapes]
        + [pltpu.SMEM((2 * GROUPS,), jnp.int32)] * 2
        + [dma(shape) for shape in semaphores],
        compiler_params=pltpu.CompilerParams(
            collective_id=0, has_side_effects=True, vmem_limit_bytes=62 << 20
        ),
        cost_estimate=pl.CostEstimate(flops=12 << 30, bytes_accessed=10 << 20, transcendentals=0),
        name="gradient_blocks",
    )(owners, acts, grads_out, left_root, right_root)


def grams_kernel(
    owned_ref, ls_ref, rs_ref, held_ref, ln_ref, rn_ref, out_ref, owned, left_stats, right_stats, held, load_sem, store_sem, held_sem
):
    loads = [
        [
            pltpu.make_async_copy(ls_ref.at[0, 0, s], left_stats.at[s], load_sem.at[s, 0]),
            pltpu.make_async_copy(rs_ref.at[0, 0, s], right_stats.at[s], load_sem.at[s, 1]),
            pltpu.make_async_copy(owned_ref.at[s], owned.at[s], load_sem.at[s, 2]),
        ]
        for s in range(CAP)
    ]
    for copies in loads:
        for copy in copies:
            copy.start()
    load_held = pltpu.make_async_copy(held_ref, held, held_sem.at[0])
    load_held.start()
    stores = [pltpu.make_async_copy(held, out_ref, held_sem.at[1])]
    for s in range(CAP):
        for copy in loads[s]:
            copy.wait()
        block = owned[s]
        sides = ((left_stats, ln_ref, 1), (right_stats, rn_ref, 0))
        for i, (stats, new_ref, dim) in enumerate(sides):
            gram = lax.dot_general(block, block, (((dim,), (dim,)), ((), ())), preferred_element_type=F32)
            stats[s] = STAT_DECAY * stats[s] + (1.0 - STAT_DECAY) * gram
            store = pltpu.make_async_copy(stats.at[s], new_ref.at[0, 0, s], store_sem.at[s, i])
            store.start()
            stores.append(store)
        if s == CAP - 2:
            load_held.wait()
            stores[0].start()
    for store in stores:
        store.wait()


def grams(owned, left_stats, right_stats, update):
    dma = pltpu.SemaphoreType.DMA
    return pl.pallas_call(
        grams_kernel,
        in_specs=[pl.BlockSpec(memory_space=pl.ANY)] * 4,
        out_specs=[pl.BlockSpec(memory_space=pl.ANY)] * 3,
        out_shape=(
            jax.ShapeDtypeStruct(left_stats.shape, F32),
            jax.ShapeDtypeStruct(right_stats.shape, F32),
            jax.ShapeDtypeStruct(update.shape, BF16),
        ),
        scratch_shapes=[
            pltpu.VMEM((CAP, BLK, BLK), BF16),
            pltpu.VMEM((CAP, BLK, BLK), F32),
            pltpu.VMEM((CAP, BLK, BLK), F32),
            pltpu.VMEM(update.shape, BF16),
            dma((CAP, 3)), dma((CAP, 2)), dma((2,)),
        ],
        compiler_params=pltpu.CompilerParams(vmem_limit_bytes=62 << 20),
        name="grams",
    )(owned, left_stats, right_stats, update)


def body(acts, grads_out, owners, left_stats, right_stats, left_root, right_root):
    owned, update = gradient_blocks(owners.reshape(-1), acts, grads_out, left_root, right_root)
    return grams(owned, left_stats, right_stats, update)


def solution(mesh):
    placed = (
        P("dp", "group"),
        P("dp", "group"),
        P("dp", None, None),
        P("dp", "group", None, None, None),
        P("dp", "group", None, None, None),
        P("dp", "group", None, None, None),
        P("dp", "group", None, None, None),
    )
    return jax.shard_map(
        body,
        mesh=mesh,
        in_specs=placed,
        out_specs=(
            P("dp", "group", None, None, None),
            P("dp", "group", None, None, None),
            P(("group", "dp"), None, None),
        ),
        check_vma=False,
    )
```

```python
import functools

import jax
import jax.numpy as jnp
from jax import lax
from jax.experimental import pallas as pl
from jax.experimental.pallas import tpu as pltpu
from jax.sharding import PartitionSpec as P

MESH = pl.DeviceIdType.MESH
STAT_DECAY = 0.9
EPSILON = 1e-06
BLK = 512
HALF = BLK // 2
SIDE = 4
GROUPS = 8
CAP = 3
QUARTER = HALF // 2
SIZES = (64, 64, 64, 64, 64, 64, 64, 64)
ROUNDS = len(SIZES)
PER_HALF = ROUNDS // 2
LARGEST = max(SIZES)
STARTS = [2 * sum(SIZES[r - r % PER_HALF : r]) for r in range(ROUNDS)]
SLOTS = 3
MERGE1, BETWEEN, MERGE2, SPREAD, PASS_ON, PASS_LAST = 0, 1, 1, 2, 2, 3
F32 = jnp.float32
BF16 = jnp.bfloat16


def place():
    dp, group = lax.axis_index("dp"), lax.axis_index("group")
    return dp // SIDE, group // 2, lax.rem(dp, SIDE), lax.rem(group, 2)


def ring(index, step):
    return lax.rem(index + step + SIDE, SIDE)


def device(x, y, z, core):
    return (x * SIDE + z, y * 2 + core)


def remote(src, dst, send, recv, target):
    return pltpu.make_async_remote_copy(
        src_ref=src, dst_ref=dst, send_sem=send, recv_sem=recv, device_id=target, device_id_type=MESH
    )


def greet(targets):
    barrier = pltpu.get_barrier_semaphore()
    for target in targets:
        pl.semaphore_signal(barrier, inc=1, device_id=target, device_id_type=MESH)
    pl.semaphore_wait(barrier, len(targets))


def plus(*terms):
    total = terms[0].astype(F32)
    for term in terms[1:]:
        total = total + term.astype(F32)
    return total.astype(BF16)


class RingSum:
    def __init__(self, parts, me, right, left, far, near, send, recv):
        self.parts, self.me, self.far, self.near = parts, me, far, near

        def copy(d, half, dst, recv_sem, target):
            return remote(parts.at[ring(me, d), half], dst, send, recv_sem, target)

        self.copies = [
            copy(2, 0, far.at[0], recv.at[0], right),
            copy(2, 1, far.at[1], recv.at[1], left),
            copy(1, 1, near.at[0, 1], recv.at[2], right),
            copy(-1, 0, near.at[1, 0], recv.at[2], left),
            copy(1, 0, near.at[0, 0], recv.at[2], right),
            copy(-1, 1, near.at[1, 1], recv.at[2], left),
        ]
        sent = parts.at[pl.ds(0, SIDE - 1)]
        self.all_sent = remote(sent, sent, send, recv.at[2], right)
        self.all_near = remote(near, near, send, recv.at[2], right)

    def first(self):
        for copy in self.copies[:4]:
            copy.start()

    def merge(self):
        for j, (step, half) in enumerate(((1, 0), (-1, 1))):
            self.copies[j].wait_recv()
            at = ring(self.me, step)
            self.parts[at, half] = plus(self.parts[at, half], self.far[j])
            self.copies[4 + j].start()

    def total(self):
        self.all_near.wait_recv()
        return [plus(self.parts[self.me, half], self.near[0, half], self.near[1, half]) for half in range(2)]

    def finish(self):
        self.all_sent.wait_send()


def gradient_kernel(
    owners, acts_ref, grads_ref, lr_ref, rr_ref,
    owned_ref, out_ref,
    grads, turned, acts, parts, far1, near1, sums, far2, near2, blocks0, blocks1,
    roots, pair_roots, roots_packed, roots_far, roots_near, holder_roots,
    result, held, packed, back_far, back_near, owned, slot_table, rank_table,
    local_sem, pair_send, pair_recv, acts_send, acts_recv, acts_cross_send, acts_cross_recv,
    send1, recv1, send2, recv2, out_send, out_recv, cross_send, cross_recv,
    swap_send, swap_recv, back_send, back_recv, roots_swap_send, roots_swap_recv, roots_send, roots_recv, owned_sem,
):
    x, y, z, core = place()
    group = y * 2 + core
    partner = device(x, y, z, 1 - core)
    along_y = [device(x, ring(y, s), z, core) for s in (1, -1)]
    along_x = [device(ring(x, s), y, z, core) for s in (1, -1)]
    along_z = [device(x, y, ring(z, s), core) for s in (1, -1)]
    blocks = (blocks0, blocks1)
    started = []

    def go(copy):
        copy.start()
        started.append(copy)
        return copy

    load_acts = pltpu.make_async_copy(acts_ref, acts.at[core, y], local_sem.at[0])
    load_grads = pltpu.make_async_copy(grads_ref, grads, local_sem.at[1])
    load_roots = [
        pltpu.make_async_copy(ref.at[0, 0], roots.at[i], local_sem.at[2 + i]) for i, ref in enumerate((lr_ref, rr_ref))
    ]
    load_acts.start()
    load_grads.start()
    for copy in load_roots:
        copy.start()
    greet([partner] + along_y + along_x + along_z)

    load_acts.wait()
    own = acts.at[core, y]
    pair = go(remote(own, own, pair_send.at[0], pair_recv.at[0], partner))
    gathers = {}

    def rows_of(h, at, start, size):
        return acts.at[h, at, pl.ds(pl.multiple_of(core * HALF + start, 16), size)]

    def acts_first(h):
        gathers[h] = []
        for i in range(2):
            for j in range(2):
                here = rows_of(h, y, (i ^ j) * QUARTER, QUARTER)
                n = 2 * i + j
                gathers[h].append(go(remote(here, here, acts_send.at[h, n], acts_recv.at[h, n], along_y[j])))
        gathers[h, "cross"] = []

    def acts_cross(h, i, at):
        here = rows_of(h, at, 0, HALF)
        gathers[h, "cross"].append(
            go(remote(here, here, acts_cross_send.at[h, i], acts_cross_recv.at[h, i], partner))
        )

    def acts_forward(h):
        for j in range(2):
            gathers[h][j].wait_recv()
            here = rows_of(h, ring(y, (-1, 1)[j]), j * QUARTER, QUARTER)
            n = 4 + j
            gathers[h].append(go(remote(here, here, acts_send.at[h, n], acts_recv.at[h, n], along_y[j])))
        for j in range(2):
            gathers[h][2 + j].wait_recv()
            acts_cross(h, j, ring(y, (-1, 1)[j]))

    def acts_last(h):
        for copy in gathers[h][4:]:
            copy.wait_recv()
        acts_cross(h, 2, ring(y, 2))

    def acts_ready(h):
        for copy in gathers[h, "cross"]:
            copy.wait_recv()

    pair.wait_recv()
    acts_first(0)

    count = 2 * GROUPS
    owner = [owners[k] for k in range(count)]
    zero, one = jnp.int32(0), jnp.int32(1)
    slot, rank = [], []
    for k in range(count):
        same = [jnp.where(owner[k2] == owner[k], one, zero) for k2 in range(k)]
        slot.append(sum(same, zero))
        rank.append(sum(same[0::2], zero))
        slot_table[k] = jnp.minimum(slot[k], CAP - 1)
        rank_table[k] = jnp.minimum(rank[k], CAP - 1)
    is_mine = [owner[k] == group for k in range(count)]

    def pick(positions, test, value):
        return sum([jnp.where(is_mine[k] & test(k), value(k), zero) for k in positions], zero)

    load_grads.wait()
    for xd in range(SIDE):
        for start in range(0, BLK, QUARTER):
            turned[xd, start : start + QUARTER, :] = grads[:, xd * BLK + start : xd * BLK + start + QUARTER].T
    acts_forward(0)
    for copy in load_roots:
        copy.wait()
    acts_last(0)
    roots_swap = go(remote(roots, pair_roots, roots_swap_send.at[0], roots_swap_recv.at[0], partner))

    stages1, stages2, outs, crosses = {}, {}, {}, {}

    def products(r):
        p, b, size = r // PER_HALF, r % SLOTS, SIZES[r]
        if r % PER_HALF == 0:
            acts_ready(p)
        for u in range(2):
            if r >= SLOTS:
                stages1[r - SLOTS, u].finish()
            left = turned[:, STARTS[r] + u * size : STARTS[r] + (u + 1) * size, :].reshape(SIDE * size, BLK)

            def step(zd, carry, u=u, left=left):
                value = jnp.dot(left, acts[p, zd], preferred_element_type=F32).astype(BF16)
                for xd in range(SIDE):
                    piece = value[xd * size : (xd + 1) * size]
                    if u == 0:
                        parts[b, 0, xd, zd // 2, lax.rem(zd, 2), 0:size] = piece
                    else:
                        parts[b, 1, zd, xd // 2, xd % 2, 0:size] = piece
                return carry

            lax.fori_loop(0, SIDE, step, 0)
            me, (right, left_to) = ((x, along_x), (z, along_z))[u]
            stage = RingSum(
                parts.at[b, u], me, right, left_to, far1.at[b, u], near1.at[b, u], send1.at[b, u], recv1.at[b, u]
            )
            stage.first()
            stages1[r, u] = stage

    def merge1(r):
        for u in range(2):
            stages1[r, u].merge()

    def between(r):
        b, size = r % SLOTS, SIZES[r] // 2
        for u in range(2):
            if r >= SLOTS:
                stages2[r - SLOTS, u].finish()
            total = stages1[r, u].total()
            for half in range(2):
                for o in range(2):
                    for piece in range(2):
                        sums[b, u, half * 2 + o, piece, 0:size] = total[half][o, piece * size : (piece + 1) * size]
            me, (right, left_to) = ((z, along_z), (x, along_x))[u]
            stage = RingSum(
                sums.at[b, u], me, right, left_to, far2.at[b, u], near2.at[b, u], send2.at[b, u], recv2.at[b, u]
            )
            stage.first()
            stages2[r, u] = stage

    def merge2(r):
        for u in range(2):
            stages2[r, u].merge()

    def strip(r, at, start, size):
        return blocks[r // PER_HALF].at[at, pl.ds(STARTS[r] + start, size)]

    def cross(r, i, at):
        here = strip(r, at, 0, 2 * SIZES[r])
        crosses[r].append(go(remote(here, here, cross_send.at[r, i], cross_recv.at[r, i], partner)))

    def spread(r):
        p, size = r // PER_HALF, SIZES[r]
        for u in range(2):
            total = stages2[r, u].total()
            for half in range(2):
                start = STARTS[r] + u * size + half * (size // 2)
                blocks[p][group, start : start + size // 2] = total[half]
        outs[r], crosses[r] = [], []
        for i in range(2):
            for j in range(2):
                here, n = strip(r, group, (i ^ j) * size, size), 2 * i + j
                outs[r].append(remote(here, here, out_send.at[r], out_recv.at[r, n], along_y[j]))
                outs[r][-1].start()
        cross(r, 0, group)

    def pass_on(r):
        for j in range(2):
            outs[r][j].wait_recv()
            here, n = strip(r, 2 * ring(y, (-1, 1)[j]) + core, j * SIZES[r], SIZES[r]), 4 + j
            outs[r].append(remote(here, here, out_send.at[r], out_recv.at[r, n], along_y[j]))
            outs[r][-1].start()
        for j in range(2):
            outs[r][2 + j].wait_recv()
            cross(r, 1 + j, 2 * ring(y, (-1, 1)[j]) + core)

    def pass_last(r):
        for copy in outs[r][4:]:
            copy.wait_recv()
        cross(r, 3, 2 * ring(y, 2) + core)

    def blocks_ready(p):
        for r in range(p * PER_HALF, (p + 1) * PER_HALF):
            for copy in crosses[r]:
                copy.wait_recv()

    def condition(left_root, block, right_root):
        shaped = jnp.dot(left_root, block, preferred_element_type=F32).astype(BF16)
        product = jnp.dot(shaped, right_root, preferred_element_type=F32)
        scaling = lax.rsqrt(jnp.mean(product * product) + EPSILON)
        return (product * scaling).astype(BF16)

    swaps = []

    def precondition():
        for j in range(CAP):
            def test(k, j=j):
                return rank[k] == j

            even = range(0, count, 2)
            which, at = pick(even, test, lambda k: jnp.int32(k // 2)), pick(even, test, lambda k: jnp.minimum(slot[k], CAP - 1))
            result[j] = condition(roots[0, at], blocks0[which], roots[1, at])
            swaps.append(go(remote(result.at[j], held.at[j], swap_send.at[j], swap_recv.at[j], partner)))

    class Routed:
        def __init__(self, parity, table, sources, packed, far, near, send, recv):
            self.parity, self.table, self.sources = parity, table, sources
            self.packed, self.far, self.near = packed, far, near
            self.order = (((2, 0), (2, 1)), ((1, 1), (-1, 0)), ((1, 0), (-1, 1)))
            landing = ((far.at[0], far.at[1]), (near.at[0, 1], near.at[1, 0]), (near.at[0, 0], near.at[1, 1]))
            self.copies = [
                remote(packed.at[i, j], landing[i][j], send.at[2 * i + j], recv.at[2 * i + j], along_y[j])
                for i in range(3)
                for j in range(2)
            ]

        def mine(self, step, half):
            k = 2 * (2 * ring(y, step) + core) + self.parity
            owner, at = owners[k], self.table[k]
            rows = pl.ds(half * HALF, HALF)
            return [
                jnp.where(lax.rem(owner, 2) == core, here(at, rows), there(at, rows)) for here, there in self.sources
            ], owner // 2

        def send(self, i):
            for j in range(2):
                for n, value in enumerate(self.mine(*self.order[i][j])[0]):
                    self.packed[i, j, n] = value
                go(self.copies[2 * i + j])

        def merge(self):
            for j in range(2):
                self.copies[j].wait_recv()
                values, at = self.mine(*self.order[2][j])
                for n, value in enumerate(values):
                    self.packed[2, j, n] = jnp.where(at == y, value, self.far[j, n])
                go(self.copies[4 + j])

        def last(self, store):
            for copy in self.copies[2:]:
                copy.wait_recv()
            for half in range(2):
                values, at = self.mine(0, half)
                from_left = at == ring(y, -1)
                if half == 0:
                    from_left = from_left | (at == ring(y, 2))
                for n, value in enumerate(values):
                    arrived = jnp.where(from_left, self.near[0, half, n], self.near[1, half, n])
                    store(n, half, jnp.where(at == y, value, arrived))

    back = Routed(
        0, rank_table, [(lambda at, rows: result[at, rows], lambda at, rows: held[at, rows])],
        packed, back_far, back_near, back_send, back_recv,
    )
    routed = [
        Routed(
            1, slot_table,
            [(lambda at, rows, n=n: roots[n, at, rows], lambda at, rows, n=n: pair_roots[n, at, rows])],
            roots_packed.at[n], roots_far.at[n], roots_near.at[n], roots_send.at[n], roots_recv.at[n],
        )
        for n in range(2)
    ]

    def store_roots(side, _, half, value):
        holder_roots[side, half * HALF : (half + 1) * HALF] = value

    def store_update(n, half, value):
        out_ref[0, half * HALF : (half + 1) * HALF] = value

    def collect(s):
        def test(k):
            return slot[k] == s

        every = range(count)
        odd = pick(every, test, lambda k: jnp.int32(k % 2))
        at = pick(every, test, lambda k: jnp.int32(k // 2))
        used = pick(every, test, lambda k: one)
        block = jnp.where(odd > 0, blocks1[at], blocks0[at])
        owned[s] = jnp.where(used > 0, block, jnp.zeros_like(block))
        copy = pltpu.make_async_copy(owned.at[s], owned_ref.at[s], owned_sem.at[s])
        copy.start()
        return copy

    half_done = PER_HALF - 1 + PASS_LAST

    def at_lag(part, lag):
        if 0 <= step - lag < ROUNDS:
            part(step - lag)

    for step in range(ROUNDS + PASS_LAST):
        at_lag(products, 0)
        at_lag(spread, SPREAD)
        at_lag(pass_last, PASS_LAST)
        at_lag(between, BETWEEN)
        if step == half_done:
            blocks_ready(0)
            precondition()
        at_lag(merge1, MERGE1)
        at_lag(merge2, MERGE2)
        if step == ROUNDS - 1 + SPREAD:
            out_ref[1] = condition(holder_roots[0], blocks1[group], holder_roots[1])
        at_lag(pass_on, PASS_ON)
        if step == 0:
            acts_first(1)
            roots_swap.wait_recv()
            routed[0].send(0)
        if step == 1:
            acts_forward(1)
            routed[0].send(1)
        if step == 2:
            acts_last(1)
            routed[0].merge()
        if step == 3:
            routed[1].send(0)
        if step == 4:
            routed[1].send(1)
        if step == 5:
            routed[1].merge()
        if step == half_done:
            for copy in swaps:
                copy.wait_recv()
            back.send(0)
            back.send(1)
        if step == ROUNDS - 1:
            for n in range(2):
                routed[n].last(functools.partial(store_roots, n))
        if step == half_done + 1:
            back.merge()
    back.last(store_update)
    blocks_ready(1)
    kept = [collect(s) for s in range(CAP)]

    for copy in started:
        copy.wait_send()
    for r in range(ROUNDS):
        sent = blocks[r // PER_HALF].at[pl.ds(0, SIDE - 1), pl.ds(STARTS[r], 2 * SIZES[r])]
        remote(sent, sent, out_send.at[r], out_recv.at[r, 0], partner).wait_send()
    for r in range(ROUNDS - SLOTS, ROUNDS):
        for u in range(2):
            stages1[r, u].finish()
            stages2[r, u].finish()
    for copy in kept:
        copy.wait()


def gradient_blocks(owners, acts, grads_out, left_root, right_root):
    dma = pltpu.SemaphoreType.DMA
    piece, small, square, half = (2, LARGEST, BLK), (LARGEST // 2, BLK), (BLK, BLK), (HALF, BLK)
    shapes = [
        (BLK, SIDE * BLK),
        (SIDE,) + square,
        (2, SIDE) + square,
        (SLOTS, 2, SIDE, 2) + piece,
        (SLOTS, 2, 2) + piece,
        (SLOTS, 2, 2, 2) + piece,
        (SLOTS, 2, SIDE, 2) + small,
        (SLOTS, 2, 2) + small,
        (SLOTS, 2, 2, 2) + small,
        (GROUPS,) + square,
        (GROUPS,) + square,
        (2, CAP) + square,
        (2, CAP) + square,
        (2, 3, 2, 1) + half,
        (2, 2, 1) + half,
        (2, 2, 2, 1) + half,
        (2,) + square,
        (CAP,) + square,
        (CAP,) + square,
        (3, 2, 1) + half,
        (2, 1) + half,
        (2, 2, 1) + half,
        (CAP,) + square,
    ]
    semaphores = [
        (4,), (1,), (1,), (2, 6), (2, 6), (2, 3), (2, 3),
        (SLOTS, 2), (SLOTS, 2, 3), (SLOTS, 2), (SLOTS, 2, 3),
        (ROUNDS,), (ROUNDS, 6), (ROUNDS, 4), (ROUNDS, 4),
        (CAP,), (CAP,), (6,), (6,), (1,), (1,), (2, 6), (2, 6), (CAP,),
    ]
    return pl.pallas_call(
        gradient_kernel,
        out_shape=(
            jax.ShapeDtypeStruct((CAP, BLK, BLK), BF16),
            jax.ShapeDtypeStruct((2, BLK, BLK), BF16),
        ),
        in_specs=[pl.BlockSpec(memory_space=pltpu.SMEM)] + [pl.BlockSpec(memory_space=pl.ANY)] * 4,
        out_specs=(pl.BlockSpec(memory_space=pl.ANY), pl.BlockSpec(memory_space=pltpu.VMEM)),
        scratch_shapes=[pltpu.VMEM(shape, BF16) for shape in shapes]
        + [pltpu.SMEM((2 * GROUPS,), jnp.int32)] * 2
        + [dma(shape) for shape in semaphores],
        compiler_params=pltpu.CompilerParams(
            collective_id=0, has_side_effects=True, vmem_limit_bytes=62 << 20
        ),
        cost_estimate=pl.CostEstimate(flops=12 << 30, bytes_accessed=10 << 20, transcendentals=0),
        name="gradient_blocks",
    )(owners, acts, grads_out, left_root, right_root)


def grams_kernel(
    owned_ref, ls_ref, rs_ref, held_ref, ln_ref, rn_ref, out_ref, owned, left_stats, right_stats, held, load_sem, store_sem, held_sem
):
    loads = [
        [
            pltpu.make_async_copy(ls_ref.at[0, 0, s], left_stats.at[s], load_sem.at[s, 0]),
            pltpu.make_async_copy(rs_ref.at[0, 0, s], right_stats.at[s], load_sem.at[s, 1]),
            pltpu.make_async_copy(owned_ref.at[s], owned.at[s], load_sem.at[s, 2]),
        ]
        for s in range(CAP)
    ]
    for copies in loads:
        for copy in copies:
            copy.start()
    load_held = pltpu.make_async_copy(held_ref, held, held_sem.at[0])
    load_held.start()
    stores = [pltpu.make_async_copy(held, out_ref, held_sem.at[1])]
    for s in range(CAP):
        for copy in loads[s]:
            copy.wait()
        block = owned[s]
        sides = ((left_stats, ln_ref, 1), (right_stats, rn_ref, 0))
        for i, (stats, new_ref, dim) in enumerate(sides):
            gram = lax.dot_general(block, block, (((dim,), (dim,)), ((), ())), preferred_element_type=F32)
            stats[s] = STAT_DECAY * stats[s] + (1.0 - STAT_DECAY) * gram
            store = pltpu.make_async_copy(stats.at[s], new_ref.at[0, 0, s], store_sem.at[s, i])
            store.start()
            stores.append(store)
        if s == CAP - 2:
            load_held.wait()
            stores[0].start()
    for store in stores:
        store.wait()


def grams(owned, left_stats, right_stats, update):
    dma = pltpu.SemaphoreType.DMA
    return pl.pallas_call(
        grams_kernel,
        in_specs=[pl.BlockSpec(memory_space=pl.ANY)] * 4,
        out_specs=[pl.BlockSpec(memory_space=pl.ANY)] * 3,
        out_shape=(
            jax.ShapeDtypeStruct(left_stats.shape, F32),
            jax.ShapeDtypeStruct(right_stats.shape, F32),
            jax.ShapeDtypeStruct(update.shape, BF16),
        ),
        scratch_shapes=[
            pltpu.VMEM((CAP, BLK, BLK), BF16),
            pltpu.VMEM((CAP, BLK, BLK), F32),
            pltpu.VMEM((CAP, BLK, BLK), F32),
            pltpu.VMEM(update.shape, BF16),
            dma((CAP, 3)), dma((CAP, 2)), dma((2,)),
        ],
        compiler_params=pltpu.CompilerParams(vmem_limit_bytes=62 << 20),
        name="grams",
    )(owned, left_stats, right_stats, update)


def body(acts, grads_out, owners, left_stats, right_stats, left_root, right_root):
    owned, update = gradient_blocks(owners.reshape(-1), acts, grads_out, left_root, right_root)
    return grams(owned, left_stats, right_stats, update)


def solution(mesh):
    placed = (
        P("dp", "group"),
        P("dp", "group"),
        P("dp", None, None),
        P("dp", "group", None, None, None),
        P("dp", "group", None, None, None),
        P("dp", "group", None, None, None),
        P("dp", "group", None, None, None),
    )
    return jax.shard_map(
        body,
        mesh=mesh,
        in_specs=placed,
        out_specs=(
            P("dp", "group", None, None, None),
            P("dp", "group", None, None, None),
            P(("group", "dp"), None, None),
        ),
        check_vma=False,
    )
```
